128 devices in a mesh: layer: 32 (over x, z, core), space: 4 (over y).
Axes of the slice: x: 4, y: 4, z: 4, core: 2. Of those that a mesh axis runs over, the one named last changes fastest.
Arguments:
- image_features: float32 [1, 64, 128, 128], P(None, None, 'space'), may hold values from -8 to 8
- output_cotangent: float32 [1, 64, 128, 128], P(None, None, 'space'), may hold values from -2.1 to 2.1
- conv_weights: bfloat16 [64, 9, 64, 64], P('layer'), may hold values from -0.25 to 0.25
Outputs:
- section_states: float32 [32, 1, 64, 128, 128], P('layer', None, None, 'space')
- start_adjoints: float32 [32, 1, 64, 128, 128], P('layer', None, None, 'space')
- weight_grads: float32 [64, 9, 64, 64], P('layer')
The draws below stay inside these ranges and needn't reach their ends.
All inputs are finite; a program needn't handle non-finite values.
Results may differ from the reference program's by a relative error of at most 0.008.
Values may be sent and summed in bfloat16 or wider, within the bound.
A program may use at most 128 MiB of HBM per device.

```python
import math
import jax
import jax.numpy as jnp
from jax import lax

C = 64
IMG = 128
BATCH = 1
LS = 2
ITERS = 2
LAYERS = 64
N_LAYER = 32


def wave_field(key, amplitudes):
    keys = jax.random.split(key, 4)
    shape = (BATCH, C, 4, 1, 1)
    row_freq = 2.0 * math.pi / IMG * jax.random.uniform(keys[0], shape, jnp.float32, 0.5, 2.5)
    col_freq = 2.0 * math.pi / IMG * jax.random.uniform(keys[1], shape, jnp.float32, 0.5, 2.5)
    row_phase = jax.random.uniform(keys[2], shape, jnp.float32, -math.pi, math.pi)
    col_phase = jax.random.uniform(keys[3], shape, jnp.float32, -math.pi, math.pi)
    rows = jnp.arange(IMG, dtype=jnp.float32)[:, None]
    cols = jnp.arange(IMG, dtype=jnp.float32)[None, :]
    terms = amplitudes * jnp.sin(row_freq * rows + row_phase) * jnp.sin(col_freq * cols + col_phase)
    return jnp.sum(terms, axis=2)


def draw_image_features(key, part):
    key = jax.random.fold_in(key, 11)
    wave_key, amp_key, rough_key = jax.random.split(key, 3)
    shape = (BATCH, C, 4, 1, 1)
    amplitudes = jnp.clip(jax.random.normal(amp_key, shape, jnp.float32), -1.5, 1.5)
    rough = jnp.clip(0.5 * jax.random.normal(rough_key, (BATCH, C, IMG, IMG), jnp.float32), -1.5, 1.5)
    return (wave_field(wave_key, amplitudes) + rough).astype(jnp.float32)


def draw_output_cotangent(key, part):
    key = jax.random.fold_in(key, 12)
    wave_key, amp_key, rough_key = jax.random.split(key, 3)
    shape = (BATCH, C, 4, 1, 1)
    amplitudes = jnp.clip(0.2 * jax.random.normal(amp_key, shape, jnp.float32), -0.4, 0.4)
    rough = jnp.clip(0.12 * jax.random.normal(rough_key, (BATCH, C, IMG, IMG), jnp.float32), -0.36, 0.36)
    return (wave_field(wave_key, amplitudes) + rough).astype(jnp.float32)


def draw_conv_weights(key, part):
    key = jax.random.fold_in(key, 13)
    base_key, noise_key = jax.random.split(key, 2)
    common_scale = 0.11 / math.sqrt(C)
    damping = 0.3 / 9.0
    base = jnp.clip(jax.random.normal(base_key, (LAYERS, C, C), jnp.float32), -4.0, 4.0)
    noise = jnp.clip(jax.random.normal(noise_key, (LAYERS, 9, C, C), jnp.float32), -4.0, 4.0)
    skew = (base - jnp.transpose(base, (0, 2, 1))) * math.sqrt(0.5)
    common = common_scale * skew - damping * jnp.eye(C, dtype=jnp.float32)[None]
    weights = common[:, None] + 0.5 * common_scale * noise
    return weights.astype(jnp.bfloat16)


def setup_inputs(seed: int = 0) -> dict:
    streams_of = jax.random.split(jax.random.key(seed), 4)
    image_features = draw_image_features(jax.random.fold_in(streams_of[3], 71), 0)
    output_cotangent = draw_output_cotangent(jax.random.fold_in(streams_of[3], 71), 0)
    conv_weights = draw_conv_weights(jax.random.fold_in(streams_of[3], 71), 0)
    return {"image_features": image_features, "output_cotangent": output_cotangent, "conv_weights": conv_weights}


horizon = 4.0
highest = lax.Precision.HIGHEST

def widen(values):
    return lax.optimization_barrier(values).astype(jnp.float32)

def pad_image(values):
    return jnp.pad(values, ((0, 0), (0, 0), (1, 1), (1, 1)))

def forward_conv(rounded, weight):
    padded = pad_image(widen(rounded))
    row_count, col_count = (rounded.shape[2], rounded.shape[3])
    summed = jnp.zeros(rounded.shape, jnp.float32)
    for tap_index in range(9):
        tap_row, tap_col = (tap_index // 3, tap_index % 3)
        summed = summed + jnp.einsum('oc,bcrw->borw', weight[tap_index].astype(jnp.float32), padded[:, :, tap_row:tap_row + row_count, tap_col:tap_col + col_count], precision=highest)
    return summed

def backward_conv(scaled, weight):
    padded = pad_image(widen(scaled))
    row_count, col_count = (scaled.shape[2], scaled.shape[3])
    summed = jnp.zeros(scaled.shape, jnp.float32)
    for tap_index in range(9):
        tap_row, tap_col = (tap_index // 3, tap_index % 3)
        summed = summed + jnp.einsum('oc,borw->bcrw', weight[tap_index].astype(jnp.float32), padded[:, :, 2 - tap_row:2 - tap_row + row_count, 2 - tap_col:2 - tap_col + col_count], precision=highest)
    return summed

def weight_grad(scaled, rounded):
    scaled_wide = widen(scaled)
    padded = pad_image(widen(rounded))
    row_count, col_count = (rounded.shape[2], rounded.shape[3])
    tap_terms = []
    for tap_index in range(9):
        tap_row, tap_col = (tap_index // 3, tap_index % 3)
        tap_terms.append(jnp.einsum('borw,bcrw->oc', scaled_wide, padded[:, :, tap_row:tap_row + row_count, tap_col:tap_col + col_count], precision=highest))
    return jnp.stack(tap_terms)

def sweep(weights, field_state, step_size):
    for layer_index in range(weights.shape[0]):
        rounded = field_state.astype(jnp.bfloat16)
        field_state = field_state + step_size * jnp.tanh(forward_conv(rounded, weights[layer_index]))
    return field_state

def adjoint_sweep(weights, field_state, adjoint, step_size, with_grads):
    stored = []
    for layer_index in range(weights.shape[0]):
        rounded = field_state.astype(jnp.bfloat16)
        tangent = jnp.tanh(forward_conv(rounded, weights[layer_index]))
        stored.append((rounded, tangent))
        field_state = field_state + step_size * tangent
    grad_list = [None] * weights.shape[0]
    for layer_index in reversed(range(weights.shape[0])):
        rounded, tangent = stored[layer_index]
        scaled = (step_size * (1.0 - tangent * tangent) * adjoint).astype(jnp.bfloat16)
        if with_grads:
            grad_list[layer_index] = weight_grad(scaled, rounded)
        adjoint = adjoint + backward_conv(scaled, weights[layer_index])
    if with_grads:
        return (adjoint, jnp.stack(grad_list))
    return adjoint

def coarse_matrix(weights, step_size):
    summed = lax.optimization_barrier(jnp.sum(weights[0].astype(jnp.float32), axis=0))
    return jnp.eye(summed.shape[0], dtype=jnp.float32) + weights.shape[0] * step_size * summed

def mix_channels(matrix, field_state):
    return jnp.einsum('oc,bcrw->borw', matrix, field_state, precision=highest)

def reference(image_features, output_cotangent, conv_weights):
    step_size = horizon / (LS * N_LAYER)
    blocks = conv_weights.reshape(N_LAYER, LS, 9, C, C)
    coarse_mats = lax.map(lambda weights: coarse_matrix(weights, step_size), blocks)
    section_starts = jnp.broadcast_to(image_features, (N_LAYER,) + image_features.shape)

    def advance(carry, entries):
        return (mix_channels(entries[0], carry) + entries[1], carry)
    for iteration in range(ITERS):
        section_ends = lax.map(lambda entries: sweep(entries[0], entries[1], step_size), (blocks, section_starts))
        residual = section_ends - lax.map(lambda entries: mix_channels(entries[0], entries[1]), (coarse_mats, section_starts))
        unused, section_starts = lax.scan(advance, image_features, (coarse_mats, residual))

    def retreat(carry, entries):
        return (mix_channels(entries[0].T, carry) + entries[1], carry)
    adjoint_ends = jnp.broadcast_to(output_cotangent, (N_LAYER,) + output_cotangent.shape)
    for iteration in range(ITERS):
        begins = lax.map(lambda entries: adjoint_sweep(entries[0], entries[1], entries[2], step_size, False), (blocks, section_starts, adjoint_ends))
        residual = begins - lax.map(lambda entries: mix_channels(entries[0].T, entries[1]), (coarse_mats, adjoint_ends))
        unused, adjoint_ends = lax.scan(retreat, output_cotangent, (coarse_mats, residual), reverse=True)
    begins, grads = lax.map(lambda entries: adjoint_sweep(entries[0], entries[1], entries[2], step_size, True), (blocks, section_starts, adjoint_ends))
    return (section_starts, begins, grads.reshape(LAYERS, 9, C, C))
```

```python
import functools

import jax
import jax.numpy as jnp
from jax import lax
from jax.experimental import pallas as pl
from jax.experimental.pallas import tpu as pltpu
from jax.sharding import PartitionSpec as P

ITERS = 2
HORIZON = 4.0
HALO = 4
MESH = pl.DeviceIdType.MESH
F32 = jnp.float32
BF16 = jnp.bfloat16


def kernel(
    nl, ns, rows, ch, cols, step_size,
    u_in, c_in, wf, wb, bb, bbt,
    states_out, adj_out, grads_out,
    u, s, c, a, a1, t0, t1, y0, y1, x0, x1, d0, d1,
    sendq, recvq, sendx, recvx, mb, mbt, grad, grecv, gsum,
    in_sem, out_sem, uh_send, uh_recv, ch_send, ch_recv,
    b_send, b_recv, bt_send, bt_recv, q_send, q_recv, x_send, x_recv, h_send, h_recv,
    g_send, g_recv, r_send, r_recv,
):
    me = lax.axis_index("layer")
    space = lax.axis_index("space")
    ext = rows + 2 * HALO
    pairs = ext // 2
    quarter = grad.shape[0] // ns
    has_up = space > 0
    has_down = space < ns - 1

    def loop(lo, hi, body):
        def step(i, carry):
            body(i)
            return carry
        lax.fori_loop(lo, hi, step, 0)

    def partner(i):
        return lax.rem(me + i, nl)

    def neighbour(i):
        return lax.rem(space + i, ns)

    in_u = pltpu.make_async_copy(u_in, u.at[pl.ds(HALO, rows)], in_sem.at[0])
    in_c = pltpu.make_async_copy(c_in, c.at[pl.ds(HALO, rows)], in_sem.at[1])
    in_u.start()
    in_c.start()

    blank = jnp.zeros((HALO, ch, cols), F32)
    for ref in (u, c):
        ref[pl.ds(0, HALO)] = blank
        ref[pl.ds(HALO + rows, HALO)] = blank
    blank16 = jnp.zeros((HALO, ch, cols), BF16)
    for ph in range(2 * ITERS):
        recvx[ph, pl.ds(0, HALO)] = blank16
        recvx[ph, pl.ds(HALO + rows, HALO)] = blank16
    for ref in (d0, d1):
        ref[pl.ds(0, HALO)] = blank16
        ref[pl.ds(HALO + rows, HALO)] = blank16
    for ref in (y0, y1):
        for e in (0, 1, 2, ext - 1, ext, ext + 1):
            ref[e] = jnp.zeros((3 * ch, cols), F32)

    barrier = pltpu.get_barrier_semaphore()

    def greet(i):
        pl.semaphore_signal(barrier, inc=1, device_id={"layer": partner(i)}, device_id_type=MESH)
    loop(1, nl, greet)

    def greet_space(i):
        pl.semaphore_signal(barrier, inc=1, device_id={"space": neighbour(i)}, device_id_type=MESH)
    loop(1, ns, greet_space)

    pl.semaphore_wait(barrier, nl - 1 + ns - 1)

    mb[me] = bb[...]
    mbt[me] = bbt[...]

    def b_copy(i, src, dst, send, recv):
        k = partner(i)
        return pltpu.make_async_remote_copy(
            src_ref=src, dst_ref=dst.at[me], send_sem=send.at[k], recv_sem=recv.at[me],
            device_id={"layer": k}, device_id_type=MESH)

    def send_b(i):
        b_copy(i, bb, mb, b_send, b_recv).start()
    loop(1, nl, send_b)

    def halo_copies(src, dst, width, send, recv, axis_space):
        up = pltpu.make_async_remote_copy(
            src_ref=src.at[pl.ds(HALO, width)], dst_ref=dst.at[pl.ds(HALO + rows, width)],
            send_sem=send.at[0], recv_sem=recv.at[1],
            device_id={"space": lax.rem(space + ns - 1, ns)}, device_id_type=MESH)
        down = pltpu.make_async_remote_copy(
            src_ref=src.at[pl.ds(HALO + rows - width, width)],
            dst_ref=dst.at[pl.ds(HALO - width, width)],
            send_sem=send.at[1], recv_sem=recv.at[0],
            device_id={"space": lax.rem(space + 1, ns)}, device_id_type=MESH)
        return up, down

    def halo_start(copies):
        up, down = copies

        @pl.when(has_up)
        def _():
            up.start()

        @pl.when(has_down)
        def _():
            down.start()

    def halo_wait(copies):
        up, down = copies

        @pl.when(has_up)
        def _():
            up.wait_send()
            down.wait_recv()

        @pl.when(has_down)
        def _():
            down.wait_send()
            up.wait_recv()

    in_u.wait()
    u_halo = halo_copies(u, u, HALO, uh_send, uh_recv, space)
    halo_start(u_halo)
    in_c.wait()
    c_halo = halo_copies(c, c, 2, ch_send, ch_recv, space)
    halo_start(c_halo)

    def send_bt(i):
        b_copy(i, bbt, mbt, bt_send, bt_recv).start()
    loop(1, nl, send_bt)

    halo_wait(u_halo)

    lane = lax.broadcasted_iota(jnp.int32, (ch, cols), 1)
    not_first = lane > 0
    not_last = lane < cols - 1

    def shifted(v):
        left = jnp.where(not_first, pltpu.roll(v, 1, 1), 0.0)
        right = jnp.where(not_last, pltpu.roll(v, cols - 1, 1), 0.0)
        return jnp.concatenate([left.astype(BF16), v.astype(BF16), right.astype(BF16)], axis=0)

    def inside(e):
        return jnp.logical_and(
            jnp.logical_or(e >= HALO, has_up), jnp.logical_or(e < HALO + rows, has_down))

    def convolve(p, low, high, weight, y, keep):
        pair = jnp.concatenate([shifted(low), shifted(high)], axis=1)
        if keep is not None:
            keep[p] = pair
        out = jnp.dot(weight, pair, preferred_element_type=F32)
        y[2 * p + 1] = out[:, :cols]
        y[2 * p + 2] = out[:, cols:]

    def gathered(y, e):
        return y[e, 0:ch] + y[e + 1, ch:2 * ch] + y[e + 2, 2 * ch:3 * ch]

    def forward_sweep(state, lo, hi, keep, finish):
        def first(p):
            convolve(p, state[2 * p], state[2 * p + 1], wf[0], y0, x0 if keep else None)
        loop(lo, hi, first)

        def second(p):
            out = []
            for e in (2 * p, 2 * p + 1):
                tangent = jnp.tanh(gathered(y0, e))
                t0[e] = tangent
                out.append(jnp.where(inside(e), state[e] + step_size * tangent, 0.0))
            convolve(p, out[0], out[1], wf[1], y1, x1 if keep else None)
        loop(lo, hi, second)
        finish()

    def start_q(ph, r):
        pltpu.make_async_remote_copy(
            src_ref=sendq.at[ph, r], dst_ref=recvq.at[ph, me],
            send_sem=q_send.at[r], recv_sem=q_recv.at[ph, me],
            device_id={"layer": r}, device_id_type=MESH).start()

    def give_q(ph, i, r, value):
        if ph % ITERS:
            value = value - sendq[ph - 1, r].astype(F32)
        rounded = value.astype(BF16)
        sendq[ph, r] = rounded

        @pl.when(i == 0)
        def _():
            recvq[ph, r] = rounded

        @pl.when(i > 0)
        def _():
            start_q(ph, r)

    def wait_q(ph):
        def one(i):
            k = partner(i)
            copy = pltpu.make_async_remote_copy(
                src_ref=sendq.at[ph, k], dst_ref=recvq.at[ph, k],
                send_sem=q_send.at[k], recv_sem=q_recv.at[ph, k],
                device_id={"layer": k}, device_id_type=MESH)
            copy.wait_send()
            copy.wait_recv()
        loop(1, nl, one)

    def scan(ph, matrices, reverse):
        def place(i):
            return nl - 1 - i if reverse else i

        def one(i, state):
            j, following = place(i), place(i + 1)
            shift = recvq[ph, j].astype(F32)
            sendx[ph, j] = state.astype(BF16)
            if ph % ITERS:
                shift = (shift + recvq[ph - 1, j].astype(F32)
                         + sendx[ph - 1, j].astype(F32) - sendx[ph - 1, following].astype(F32))
            high = state.astype(BF16)
            low = (state - high.astype(F32)).astype(BF16)
            matrix = matrices[j]
            mixed = jnp.dot(
                jnp.concatenate([matrix, matrix], axis=1),
                jnp.concatenate([high, high, low, low], axis=0), preferred_element_type=F32)
            return state + mixed + shift
        state = lax.fori_loop(0, nl - 1, one, jnp.zeros((ch, cols), F32))
        sendx[ph, place(nl - 1)] = state.astype(BF16)

        recvx[ph, HALO + me] = sendx[ph, me]

        def give(i):
            x_copy(ph, partner(i), me).start()
        loop(1, nl, give)

    def x_copy(ph, k, row):
        return pltpu.make_async_remote_copy(
            src_ref=sendx.at[ph, k], dst_ref=recvx.at[ph, HALO + row],
            send_sem=x_send.at[k], recv_sem=x_recv.at[ph, row],
            device_id={"layer": k}, device_id_type=MESH)

    def wait_x(ph, width):
        def take(k):
            @pl.when(k != me)
            def _():
                x_copy(ph, k, k).wait_recv()
        loop(0, HALO, take)
        loop(rows - HALO, rows, take)
        copies = halo_copies(recvx.at[ph], recvx.at[ph], width, h_send.at[ph], h_recv.at[ph], space)
        halo_start(copies)
        loop(HALO, rows - HALO, take)

        def sent(i):
            k = partner(i)
            x_copy(ph, k, k).wait_send()
        loop(1, nl, sent)
        halo_wait(copies)

    for iteration in range(ITERS):
        ph = iteration

        def finish(ph=ph):
            def one(i):
                r = partner(i)
                e = r + HALO
                tangent = jnp.tanh(gathered(y1, e))
                give_q(ph, i, r, step_size * (t0[e] + tangent))
            loop(0, nl, one)
        forward_sweep(u if iteration == 0 else s, 1, pairs - 1, False, finish)
        wait_q(ph)
        if iteration == 0:
            def settle_b(i):
                k = partner(i)
                for src, dst, send, recv in ((bb, mb, b_send, b_recv), (bbt, mbt, bt_send, bt_recv)):
                    copy = pltpu.make_async_remote_copy(
                        src_ref=src, dst_ref=dst.at[k], send_sem=send.at[k], recv_sem=recv.at[k],
                        device_id={"layer": k}, device_id_type=MESH)
                    copy.wait_send()
                    copy.wait_recv()
            loop(1, nl, settle_b)
        scan(ph, mb, False)
        wait_x(ph, HALO)
        before = u if iteration == 0 else s

        def update(e, ph=ph, before=before):
            s[e] = before[e] + recvx[ph, e].astype(F32)
        loop(0, ext, update)

    states = pltpu.make_async_copy(s.at[pl.ds(HALO, rows)], states_out, out_sem.at[0])
    states.start()
    halo_wait(c_halo)

    def finish_last():
        def one(p):
            for e in (2 * p, 2 * p + 1):
                t1[e] = jnp.tanh(gathered(y1, e))
        loop(1, pairs - 1, one)
    forward_sweep(s, 0, pairs, True, finish_last)

    def adjoint_sweep(state, keep, finish):
        def scaled(tangent, value):
            return step_size * (1.0 - tangent * tangent) * value

        def first(p):
            out = []
            for e in (2 * p, 2 * p + 1):
                value = scaled(t1[e], state[e])
                if keep:
                    d1[e] = value.astype(BF16)
                out.append(value)
            convolve(p, out[0], out[1], wb[1], y0, None)
        loop(1, pairs - 1, first)

        def second(p):
            out = []
            for e in (2 * p, 2 * p + 1):
                after = state[e] + gathered(y0, e)
                a1[e] = after
                value = jnp.where(inside(e), scaled(t0[e], after), 0.0)
                if keep:
                    d0[e] = value.astype(BF16)
                out.append(value)
            convolve(p, out[0], out[1], wb[0], y1, None)
        loop(1, pairs - 1, second)
        finish()

    for iteration in range(ITERS):
        ph = ITERS + iteration

        def finish_adjoint(ph=ph):
            def one(i):
                r = partner(i)
                e = r + HALO
                give_q(ph, i, r, gathered(y0, e) + gathered(y1, e))
            loop(0, nl, one)
        before = c if iteration == 0 else a
        adjoint_sweep(before, False, finish_adjoint)
        wait_q(ph)
        scan(ph, mbt, True)
        wait_x(ph, 2)

        def update_adjoint(e, ph=ph, before=before):
            a[e] = before[e] + recvx[ph, e].astype(F32)
        loop(0, ext, update_adjoint)

    def finish_start():
        def one(e):
            a1[e] = a1[e] + gathered(y1, e)
        loop(HALO, HALO + rows, one)
    adjoint_sweep(a, True, finish_start)
    starts = pltpu.make_async_copy(a1.at[pl.ds(HALO, rows)], adj_out, out_sem.at[1])
    starts.start()

    for ref in (d0, d1):
        ref[pl.ds(0, HALO)] = blank16
        ref[pl.ds(HALO + rows, HALO)] = blank16
    for index, (d, x) in enumerate(((d0, x0), (d1, x1))):
        part = pl.ds(index * 3 * ch, 3 * ch)
        grad[part] = jnp.zeros((3 * ch, 3 * ch), F32)

        def add(p, d=d, x=x, part=part):
            e = 2 * p
            left = jnp.concatenate([d[e + 1], d[e], d[e - 1]], axis=0)
            right = jnp.concatenate([d[e + 2], d[e + 1], d[e]], axis=0)
            grad[part] += lax.dot_general(
                jnp.concatenate([left, right], axis=1), x[p], (((1,), (1,)), ((), ())),
                preferred_element_type=F32)
        loop(1, pairs - 1, add)

    def g_copy(i):
        k = neighbour(i)
        return pltpu.make_async_remote_copy(
            src_ref=grad.at[pl.ds(k * quarter, quarter)], dst_ref=grecv.at[space],
            send_sem=g_send.at[k], recv_sem=g_recv.at[space],
            device_id={"space": k}, device_id_type=MESH)

    def g_arrival(i):
        k = neighbour(i)
        return pltpu.make_async_remote_copy(
            src_ref=grad.at[pl.ds(k * quarter, quarter)], dst_ref=grecv.at[k],
            send_sem=g_send.at[k], recv_sem=g_recv.at[k],
            device_id={"space": k}, device_id_type=MESH)

    for i in range(1, ns):
        g_copy(i).start()
    total = grad[pl.ds(pl.multiple_of(space * quarter, quarter), quarter)]
    for i in range(1, ns):
        g_arrival(i).wait_recv()
        total = total + grecv[neighbour(i)]
    own = pl.ds(pl.multiple_of(space * quarter, quarter), quarter)
    gsum[own] = total

    def r_copy(i, source):
        k = neighbour(i)
        part = pl.ds(source * quarter, quarter)
        return pltpu.make_async_remote_copy(
            src_ref=gsum.at[part], dst_ref=gsum.at[part],
            send_sem=r_send.at[k], recv_sem=r_recv.at[source],
            device_id={"space": k}, device_id_type=MESH)

    for i in range(1, ns):
        r_copy(i, space).start()
    for i in range(1, ns):
        g_arrival(i).wait_send()
        r_copy(i, neighbour(i)).wait_recv()
        r_copy(i, space).wait_send()
    grads = pltpu.make_async_copy(gsum, grads_out, out_sem.at[2])
    grads.start()
    states.wait()
    starts.wait()
    grads.wait()


def split(matrix):
    high = matrix.astype(BF16)
    low = (matrix - high.astype(F32)).astype(BF16)
    return jnp.concatenate([high, low], axis=1)


def per_device(image_features, output_cotangent, conv_weights):
    nl, ns = lax.axis_size("layer"), lax.axis_size("space")
    layers, _, ch, _ = conv_weights.shape
    _, _, rows, cols = image_features.shape
    assert rows == nl and layers == 2 and cols == 2 * ch
    step_size = HORIZON / (layers * nl)
    ext = rows + 2 * HALO

    taps = conv_weights.reshape(layers, 3, 3, ch, ch)
    wf = taps.transpose(0, 1, 3, 2, 4).reshape(layers, 3 * ch, 3 * ch)
    wb = taps[:, ::-1, ::-1].transpose(0, 1, 4, 2, 3).reshape(layers, 3 * ch, 3 * ch)
    coarse = layers * step_size * jnp.sum(conv_weights[0].astype(F32), axis=0)

    u_in = image_features[0].transpose(1, 0, 2)
    c_in = output_cotangent[0].transpose(1, 0, 2)

    field = functools.partial(pltpu.VMEM, (ext, ch, cols))
    any_spec = pl.BlockSpec(memory_space=pl.ANY)
    vmem_spec = pl.BlockSpec(memory_space=pltpu.VMEM)
    dma = pltpu.SemaphoreType.DMA
    phases = 2 * ITERS
    states, starts, grads = pl.pallas_call(
        functools.partial(kernel, nl, ns, rows, ch, cols, step_size),
        out_shape=(
            jax.ShapeDtypeStruct((rows, ch, cols), F32),
            jax.ShapeDtypeStruct((rows, ch, cols), F32),
            jax.ShapeDtypeStruct((layers * 3 * ch, 3 * ch), F32),
        ),
        in_specs=[any_spec, any_spec, vmem_spec, vmem_spec, vmem_spec, vmem_spec],
        out_specs=(any_spec, any_spec, any_spec),
        scratch_shapes=[
            field(F32), field(F32), field(F32), field(F32), field(F32), field(F32), field(F32),
            pltpu.VMEM((ext + 2, 3 * ch, cols), F32),
            pltpu.VMEM((ext + 2, 3 * ch, cols), F32),
            pltpu.VMEM((ext // 2, 3 * ch, 2 * cols), BF16),
            pltpu.VMEM((ext // 2, 3 * ch, 2 * cols), BF16),
            field(BF16), field(BF16),
            pltpu.VMEM((phases, rows, ch, cols), BF16),
            pltpu.VMEM((phases, nl, ch, cols), BF16),
            pltpu.VMEM((phases, nl, ch, cols), BF16),
            pltpu.VMEM((phases, ext, ch, cols), BF16),
            pltpu.VMEM((nl, ch, 2 * ch), BF16),
            pltpu.VMEM((nl, ch, 2 * ch), BF16),
            pltpu.VMEM((layers * 3 * ch, 3 * ch), F32),
            pltpu.VMEM((ns, layers * 3 * ch // ns, 3 * ch), F32),
            pltpu.VMEM((layers * 3 * ch, 3 * ch), F32),
            dma((2,)), dma((3,)), dma((2,)), dma((2,)), dma((2,)), dma((2,)),
            dma((nl,)), dma((nl,)), dma((nl,)), dma((nl,)),
            dma((nl,)), dma((phases, nl)), dma((nl,)), dma((phases, nl)),
            dma((phases, 2)), dma((phases, 2)),
            dma((ns,)), dma((ns,)), dma((ns,)), dma((ns,)),
        ],
        compiler_params=pltpu.CompilerParams(
            collective_id=0, has_side_effects=True, vmem_limit_bytes=56 * 1024 * 1024),
        name="mgrit",
    )(u_in, c_in, wf, wb, split(coarse), split(coarse.T))

    grads = grads.reshape(layers, 3, ch, 3, ch).transpose(0, 1, 3, 2, 4)
    return (
        states.transpose(1, 0, 2)[None, None],
        starts.transpose(1, 0, 2)[None, None],
        grads.reshape(layers, 9, ch, ch),
    )


def solution(mesh):
    placed = (
        P(None, None, "space", None),
        P(None, None, "space", None),
        P("layer", None, None, None),
    )
    return jax.shard_map(
        per_device,
        mesh=mesh,
        in_specs=placed,
        out_specs=(
            P("layer", None, None, "space", None),
            P("layer", None, None, "space", None),
            P("layer", None, None, None),
        ),
        check_vma=False,
    )
```

```python
import functools

import jax
import jax.numpy as jnp
from jax import lax
from jax.experimental import pallas as pl
from jax.experimental.pallas import tpu as pltpu
from jax.sharding import PartitionSpec as P

ITERS = 2
HORIZON = 4.0
HALO = 4
GROUP = 4
MESH = pl.DeviceIdType.MESH
F32 = jnp.float32
BF16 = jnp.bfloat16


def kernel(
    nl, ns, rows, ch, cols, step_size,
    u_in, c_in, w_in,
    states_out, adj_out, grads_out,
    u, s, c, a, a1, t0, t1, y0, y1, x0, x1, d0, d1,
    sendq, recvq, sendx, recvx, w, wf, wb, mb, rev_m, fwd_p, rev_p, ys,
    grad, grecv, gsum, gout,
    in_sem, out_sem, uh_send, uh_recv, ch_send, ch_recv,
    b_send, b_recv, q_send, q_recv, x_send, x_recv, h_send, h_recv,
    g_send, g_recv, r_send, r_recv,
):
    me = lax.axis_index("layer")
    space = lax.axis_index("space")
    ext = rows + 2 * HALO
    pairs = ext // 2
    own = rows // 2
    groups = nl // GROUP
    has_up = space > 0
    has_down = space < ns - 1

    def loop(lo, hi, body):
        def step(i, carry):
            body(i)
            return carry
        lax.fori_loop(lo, hi, step, 0)

    def partner(i):
        return lax.rem(me + i, nl)

    def neighbour(i):
        return lax.rem(space + i, ns)

    in_w = pltpu.make_async_copy(w_in, w, in_sem.at[2])
    in_w.start()
    for r in range(rows):
        pltpu.make_async_copy(u_in.at[:, r, 0], u.at[HALO + r], in_sem.at[0]).start()
    for r in range(rows):
        pltpu.make_async_copy(c_in.at[:, r, 0], c.at[HALO + r], in_sem.at[1]).start()

    def own_rows(ref):
        return ref.at[pl.ds(HALO, rows)]

    blank = jnp.zeros((HALO, ch, cols), F32)
    for ref in (u, c):
        ref[pl.ds(0, HALO)] = blank
        ref[pl.ds(HALO + rows, HALO)] = blank
    blank16 = jnp.zeros((HALO, ch, cols), BF16)
    for ph in range(2 * ITERS):
        recvx[ph, pl.ds(0, HALO)] = blank16
        recvx[ph, pl.ds(HALO + rows, HALO)] = blank16

    barrier = pltpu.get_barrier_semaphore()

    def greet(i):
        pl.semaphore_signal(barrier, inc=1, device_id={"layer": partner(i)}, device_id_type=MESH)
    loop(1, nl, greet)

    def greet_space(i):
        pl.semaphore_signal(barrier, inc=1, device_id={"space": neighbour(i)}, device_id_type=MESH)
    loop(1, ns, greet_space)

    for ref in (y0, y1):
        for e in (0, 1, 2, ext - 1, ext, ext + 1):
            ref[e] = jnp.zeros((3 * ch, cols), F32)

    def halves(matrix):
        high = matrix.astype(BF16)
        low = (matrix - high.astype(F32)).astype(BF16)
        return jnp.concatenate([high, low], axis=1)

    in_w.wait()
    summed = w[0, 0].astype(F32)
    for tap in range(1, 9):
        summed = summed + w[0, tap].astype(F32)
    mb[me] = halves(2 * step_size * summed)
    for layer in range(2):
        for ty in range(3):
            wf[layer, ty * ch:(ty + 1) * ch] = jnp.concatenate(
                [w[layer, 3 * ty + tx] for tx in range(3)], axis=1)

    pltpu.make_async_copy(own_rows(u), own_rows(u), in_sem.at[0]).wait()
    pl.semaphore_wait(barrier, nl - 1 + ns - 1)

    def b_copy(i, source):
        k = partner(i)
        return pltpu.make_async_remote_copy(
            src_ref=mb.at[source], dst_ref=mb.at[source], send_sem=b_send.at[k],
            recv_sem=b_recv.at[source], device_id={"layer": k}, device_id_type=MESH)

    up_device = {"space": lax.rem(space + ns - 1, ns)}
    down_device = {"space": lax.rem(space + 1, ns)}

    def edge_copies(ref, width, send, recv):
        up = pltpu.make_async_remote_copy(
            src_ref=ref.at[pl.ds(HALO, width)], dst_ref=ref.at[pl.ds(HALO + rows, width)],
            send_sem=send.at[0], recv_sem=recv.at[1], device_id=up_device, device_id_type=MESH)
        down = pltpu.make_async_remote_copy(
            src_ref=ref.at[pl.ds(HALO + rows - width, width)],
            dst_ref=ref.at[pl.ds(HALO - width, width)],
            send_sem=send.at[1], recv_sem=recv.at[0], device_id=down_device, device_id_type=MESH)
        return up, down

    def edge_start(copies):
        up, down = copies
        pl.when(has_up)(up.start)
        pl.when(has_down)(down.start)

    def edge_wait(copies):
        up, down = copies

        @pl.when(has_up)
        def _():
            up.wait_send()
            down.wait_recv()

        @pl.when(has_down)
        def _():
            down.wait_send()
            up.wait_recv()

    edge_start(edge_copies(u, HALO, uh_send, uh_recv))

    def send_b(i):
        b_copy(i, me).start()
    loop(1, nl, send_b)

    lane = lax.broadcasted_iota(jnp.int32, (ch, cols), 1)
    not_first = lane > 0
    not_last = lane < cols - 1

    def shifted(v):
        left = jnp.where(not_first, pltpu.roll(v, 1, 1), 0.0)
        right = jnp.where(not_last, pltpu.roll(v, cols - 1, 1), 0.0)
        return jnp.concatenate([left.astype(BF16), v.astype(BF16), right.astype(BF16)], axis=0)

    def inside(e):
        return jnp.logical_and(
            jnp.logical_or(e >= HALO, has_up), jnp.logical_or(e < HALO + rows, has_down))

    def convolve(which, value, weight, y, keep=None):
        matrix = weight[...]
        values = [(value(2 * p), value(2 * p + 1)) for p in which]
        stacked = [
            jnp.concatenate([shifted(low), shifted(high)], axis=1) for low, high in values]
        products = [jnp.dot(matrix, x, preferred_element_type=F32) for x in stacked]
        for p, x, product in zip(which, stacked, products):
            if keep is not None:
                keep[p] = x
            y[2 * p + 1] = product[:, :cols]
            y[2 * p + 2] = product[:, cols:]

    def gathered(y, e):
        return y[e, 0:ch] + y[e + 1, ch:2 * ch] + y[e + 2, 2 * ch:3 * ch]

    def q_copy(ph, r, source):
        return pltpu.make_async_remote_copy(
            src_ref=sendq.at[ph, r], dst_ref=recvq.at[ph, source],
            send_sem=q_send.at[r], recv_sem=q_recv.at[ph, source],
            device_id={"layer": r}, device_id_type=MESH)

    def give_q(ph, which, value):
        for p in which:
            for e in (2 * p, 2 * p + 1):
                r = e - HALO
                entry = value(e)
                if ph % ITERS:
                    entry = entry - sendq[ph - 1, r].astype(F32)
                sendq[ph, r] = entry.astype(BF16)
        for p in which:
            for r in (2 * p - HALO, 2 * p + 1 - HALO):
                pl.when(r != me)(lambda r=r: q_copy(ph, r, me).start())

    def wait_q_sent(ph):
        def one(i):
            q_copy(ph, partner(i), me).wait_send()
        loop(1, nl, one)

    def x_copy(ph, k, row):
        return pltpu.make_async_remote_copy(
            src_ref=sendx.at[ph, k], dst_ref=recvx.at[ph, HALO + row],
            send_sem=x_send.at[k], recv_sem=x_recv.at[ph, row],
            device_id={"layer": k}, device_id_type=MESH)

    def wait_x_sent(ph):
        def one(i):
            x_copy(ph, partner(i), me).wait_send()
        loop(1, nl, one)

    def halo_copies(ph, far):
        def one(index, source, target, device):
            return pltpu.make_async_remote_copy(
                src_ref=recvx.at[ph, pl.ds(source, 2)], dst_ref=recvx.at[ph, pl.ds(target, 2)],
                send_sem=h_send.at[ph, index], recv_sem=h_recv.at[ph, index],
                device_id=device, device_id_type=MESH)
        last = HALO + rows
        up = [(0, one(0, HALO, last, up_device))]
        down = [(own - 1, one(2, last - 2, HALO - 2, down_device))]
        if far:
            up.append((1, one(1, HALO + 2, last + 2, up_device)))
            down.append((own - 2, one(3, last - 4, HALO - 4, down_device)))
        return up, down

    def sweep(arrival, far, edge, first_value, first_weight, second_value, second_weight,
              finish, keeps=(None, None), middle=None, spread=False):
        start = lax.div(lax.rem(me + nl - 1, nl), 2)

        def begin(m):
            places = [lax.rem(start + own - 2 * m - k, own) for k in range(2)]
            if arrival is not None:
                up, down = halo_copies(arrival, far)
                for place in places:
                    for row in (2 * place, 2 * place + 1):
                        pl.when(row != me)(
                            lambda row=row: x_copy(arrival, row, row).wait_recv())
                    for at, copy in up:
                        pl.when(jnp.logical_and(place == at, has_up))(copy.start)
                    for at, copy in down:
                        pl.when(jnp.logical_and(place == at, has_down))(copy.start)
            convolve([HALO // 2 + place for place in places],
                     first_value, first_weight, y0, keeps[0])
        loop(0, own // 2, begin)
        if arrival is None:
            edge_wait(edge)
        else:
            up, down = halo_copies(arrival, far)

            @pl.when(has_up)
            def _():
                for at, copy in up:
                    copy.wait_send()
                for at, copy in down:
                    copy.wait_recv()

            @pl.when(has_down)
            def _():
                for at, copy in down:
                    copy.wait_send()
                for at, copy in up:
                    copy.wait_recv()
        if spread:
            convolve([0, 1, pairs - 2, pairs - 1], first_value, first_weight, y0, keeps[0])
        else:
            convolve([1, pairs - 2], first_value, first_weight, y0, keeps[0])
            if far:
                for e in (0, 1, ext - 2, ext - 1):
                    first_value(e)
        if middle is not None:
            middle()

        def ring(n):
            return HALO // 2 + lax.rem(lax.div(me, 2) + own - 1 + n, own)
        outer = [0, 1, pairs - 2, pairs - 1] if spread else [1, pairs - 2]
        convolve(outer, second_value, second_weight, y1, keeps[1])
        convolve([ring(0), ring(1)], second_value, second_weight, y1, keeps[1])
        convolve([ring(2), ring(3)], second_value, second_weight, y1, keeps[1])

        def more(m):
            finish([ring(2 * m - 3), ring(2 * m - 2)])
            convolve([ring(2 * m), ring(2 * m + 1)], second_value, second_weight, y1, keeps[1])
        loop(2, own // 2, more)
        finish([ring(own - 3), ring(own - 2)])
        finish([ring(own - 1), ring(0)])

    def mixed(matrices, state):
        high = state.astype(BF16)
        low = (state - high.astype(F32)).astype(BF16)
        return jnp.dot(
            jnp.concatenate([matrices, matrices], axis=1),
            jnp.concatenate([high, high, low, low], axis=0), preferred_element_type=F32)

    def prepare(matrices, products):
        def one(g):
            total = [None] * 2
            for k in range(GROUP):
                for t in range(2):
                    at = GROUP * (2 * g + t) + k
                    matrix = matrices[at]
                    plain = matrix[:, :ch].astype(F32) + matrix[:, ch:].astype(F32)
                    if k == 0:
                        total[t] = plain
                    else:
                        total[t] = total[t] + plain + mixed(matrix, total[t])
                    products[2 * g + t, pl.ds(k * ch, ch)] = halves(total[t])
        loop(0, groups // 2, one)

    def scan(ph, matrices, products, reverse):
        blocks = groups // 2
        size = 2 * GROUP

        def section(i):
            return nl - 1 - i if reverse else i

        def shift(i):
            j = section(i)
            value = recvq[ph, j].astype(F32)
            if ph % ITERS:
                following = section(jnp.minimum(i + 1, nl - 1))
                value = (value + recvq[ph - 1, j].astype(F32)
                         + sendx[ph - 1, j].astype(F32) - sendx[ph - 1, following].astype(F32))
            return value

        def within(n):
            block = lax.rem(lax.div(lax.rem(me + nl - 1, nl), size) + 2 * blocks - 1 - n, blocks)

            def arrive(k):
                j = block * size + k
                pl.when(j != me)(lambda: q_copy(ph, j, j).wait_recv())
            loop(0, size, arrive)
            if reverse:
                block = blocks - 1 - block
            state = [None] * 2
            for k in range(GROUP):
                for t in range(2):
                    i = block * size + t * GROUP + k
                    value = shift(i)
                    if k > 0:
                        value = value + state[t] + mixed(matrices[i], state[t])
                    state[t] = value
                    ys[i] = value
        loop(0, blocks, within)

        entering = [jnp.zeros((ch, cols), F32), ys[GROUP - 1]]
        for g in range(1, groups - 1):
            state = entering[g]
            entering.append(
                ys[GROUP * g + GROUP - 1] + state
                + mixed(products[g, pl.ds((GROUP - 1) * ch, ch)], state))
        for g in range(groups):
            ys[GROUP * g + GROUP - 1] = entering[g]

        def spread_group(n):
            targets = []
            for t in range(2):
                g = lax.rem(lax.div(me, GROUP) + 2 * n + t, groups)
                if reverse:
                    g = groups - 1 - g
                state = ys[GROUP * g + GROUP - 1]
                change = mixed(products[g, pl.ds(0, (GROUP - 1) * ch)], state)
                results = [state]
                for k in range(GROUP - 1):
                    results.append(ys[GROUP * g + k] + state + change[k * ch:(k + 1) * ch])
                for k in range(GROUP):
                    j = section(GROUP * g + k)
                    sendx[ph, j] = results[k].astype(BF16)
                    targets.append(j)
            for j in targets:
                pl.when(j != me)(lambda j=j: x_copy(ph, j, me).start())
        loop(0, groups // 2, spread_group)
        recvx[ph, HALO + me] = sendx[ph, me]

    c_edge = edge_copies(c, 2, ch_send, ch_recv)

    def forward_first(ph, before):
        def value(e):
            if ph is None:
                return u[e]
            new = before[e] + recvx[ph, e].astype(F32)
            s[e] = new
            return new
        return value

    def forward_second(state):
        def value(e):
            tangent = jnp.tanh(gathered(y0, e))
            t0[e] = tangent
            return jnp.where(inside(e), state[e] + step_size * tangent, 0.0)
        return value

    def finish_forward(ph):
        def value(e):
            return step_size * (t0[e] + jnp.tanh(gathered(y1, e)))
        return lambda which: give_q(ph, which, value)

    sweep(None, False, edge_copies(u, HALO, uh_send, uh_recv), forward_first(None, None),
          wf.at[0], forward_second(u), wf.at[1], finish_forward(0))
    recvq[0, me] = sendq[0, me]

    pltpu.make_async_copy(own_rows(c), own_rows(c), in_sem.at[1]).wait()
    edge_start(c_edge)

    def settle_b(i):
        b_copy(i, me).wait_send()
        b_copy(i, partner(i)).wait_recv()
    loop(1, nl, settle_b)
    prepare(mb, fwd_p)
    scan(0, mb, fwd_p, False)
    wait_q_sent(0)

    sweep(0, True, None, forward_first(0, u), wf.at[0], forward_second(s), wf.at[1],
          finish_forward(1))
    recvq[1, me] = sendq[1, me]
    wait_x_sent(0)
    scan(1, mb, fwd_p, False)
    wait_q_sent(1)

    for layer in range(2):
        for ty in range(3):
            wb[layer, ty * ch:(ty + 1) * ch] = jnp.concatenate(
                [w[layer, 8 - 3 * ty - tx].astype(F32).T for tx in range(3)], axis=1).astype(BF16)

    def transpose_b(i):
        matrix = mb[nl - 1 - i].astype(F32).T
        rev_m[i] = jnp.concatenate([matrix[:ch], matrix[ch:]], axis=1).astype(BF16)
    loop(0, nl, transpose_b)
    prepare(rev_m, rev_p)

    def finish_last(which):
        for p in which:
            for e in (2 * p, 2 * p + 1):
                t1[e] = jnp.tanh(gathered(y1, e))
    sweep(1, True, None, forward_first(1, s), wf.at[0], forward_second(s), wf.at[1],
          finish_last, keeps=(x0, x1), spread=True)
    finish_last([1, pairs - 2])
    wait_x_sent(1)
    for r in range(rows):
        pltpu.make_async_copy(s.at[HALO + r], states_out.at[:, r, 0], out_sem.at[0]).start()

    def scaled(tangent, value):
        return step_size * (1.0 - tangent * tangent) * value

    def adjoint_first(ph, before, keep):
        def value(e):
            if ph is None:
                new = c[e]
            else:
                new = before[e] + recvx[ph, e].astype(F32)
                a[e] = new
            new = scaled(t1[e], new)
            if keep:
                d1[e] = new.astype(BF16)
            return new
        return value

    def adjoint_second(state, keep):
        def value(e):
            after = state[e] + gathered(y0, e)
            if keep:
                a1[e] = after
            new = jnp.where(inside(e), scaled(t0[e], after), 0.0)
            if keep:
                d0[e] = new.astype(BF16)
            return new
        return value

    def finish_adjoint(ph):
        def value(e):
            return gathered(y0, e) + gathered(y1, e)
        return lambda which: give_q(ph, which, value)

    sweep(None, False, c_edge, adjoint_first(None, None, False), wb.at[1],
          adjoint_second(c, False), wb.at[0], finish_adjoint(2))
    recvq[2, me] = sendq[2, me]
    scan(2, rev_m, rev_p, True)
    wait_q_sent(2)
    sweep(2, False, None, adjoint_first(2, c, False), wb.at[1],
          adjoint_second(a, False), wb.at[0], finish_adjoint(3))
    recvq[3, me] = sendq[3, me]
    wait_x_sent(2)
    scan(3, rev_m, rev_p, True)
    wait_q_sent(3)

    quarter = 3 * ch // ns

    def gradient(layer, d, x):
        d[pl.ds(0, HALO)] = blank16
        d[pl.ds(HALO + rows, HALO)] = blank16

        def one(m, total):
            which = [1 + 3 * m + k for k in range(3)]
            left, right = [], []
            for p in which:
                for e in (2 * p, 2 * p + 1):
                    left.append(jnp.concatenate([d[e + 1], d[e], d[e - 1]], axis=0))
                right.append(x[p])
            return total + lax.dot_general(
                jnp.concatenate(left, axis=1), jnp.concatenate(right, axis=1),
                (((1,), (1,)), ((), ())), preferred_element_type=F32)
        grad[layer] = lax.fori_loop(
            0, (pairs - 2) // 3, one, jnp.zeros((3 * ch, 3 * ch), F32))
        for i in range(1, ns):
            g_copy(layer, i, space).start()

    def part(index):
        return pl.ds(pl.multiple_of(index * quarter, quarter), quarter)

    def g_copy(layer, i, source):
        k = neighbour(i)
        return pltpu.make_async_remote_copy(
            src_ref=grad.at[layer, part(k)], dst_ref=grecv.at[layer, source],
            send_sem=g_send.at[layer, k], recv_sem=g_recv.at[layer, source],
            device_id={"space": k}, device_id_type=MESH)

    def r_copy(layer, i, source):
        k = neighbour(i)
        return pltpu.make_async_remote_copy(
            src_ref=gsum.at[layer, part(source)], dst_ref=gsum.at[layer, part(source)],
            send_sem=r_send.at[layer, k], recv_sem=r_recv.at[layer, source],
            device_id={"space": k}, device_id_type=MESH)

    def reduce_part(layer):
        total = grad[layer, part(space)]
        for i in range(1, ns):
            g_copy(layer, i, neighbour(i)).wait_recv()
            total = total + grecv[layer, neighbour(i)]
        gsum[layer, part(space)] = total
        for i in range(1, ns):
            r_copy(layer, i, space).start()

    def collect(layer):
        for i in range(1, ns):
            g_copy(layer, i, space).wait_send()
            r_copy(layer, i, neighbour(i)).wait_recv()
            r_copy(layer, i, space).wait_send()
        for ty in range(3):
            for tx in range(3):
                gout[9 * layer + 3 * ty + tx] = (
                    gsum[layer, ty * ch:(ty + 1) * ch, tx * ch:(tx + 1) * ch])

    def finish_start(which):
        for p in which:
            for e in (2 * p, 2 * p + 1):
                a1[e] = a1[e] + gathered(y1, e)

    sweep(3, False, None, adjoint_first(3, a, True), wb.at[1], adjoint_second(a, True), wb.at[0],
          finish_start, middle=lambda: gradient(1, d1, x1))
    for r in range(rows):
        pltpu.make_async_copy(a1.at[HALO + r], adj_out.at[:, r, 0], out_sem.at[1]).start()
    gradient(0, d0, x0)
    wait_x_sent(3)
    reduce_part(1)
    reduce_part(0)
    collect(1)
    collect(0)
    grads = pltpu.make_async_copy(gout, grads_out, out_sem.at[2])
    grads.start()
    pltpu.make_async_copy(own_rows(s), own_rows(s), out_sem.at[0]).wait()
    pltpu.make_async_copy(own_rows(a1), own_rows(a1), out_sem.at[1]).wait()
    grads.wait()


def per_device(image_features, output_cotangent, conv_weights):
    nl, ns = lax.axis_size("layer"), lax.axis_size("space")
    layers, _, ch, _ = conv_weights.shape
    _, _, rows, cols = image_features.shape
    assert rows == nl and layers == 2 and cols == 2 * ch
    step_size = HORIZON / (layers * nl)
    ext = rows + 2 * HALO
    vmem = pltpu.VMEM

    def field(kind):
        return vmem((ext, ch, cols), kind)
    any_spec = pl.BlockSpec(memory_space=pl.ANY)
    dma = pltpu.SemaphoreType.DMA
    phases = 2 * ITERS
    states, starts, grads = pl.pallas_call(
        functools.partial(kernel, nl, ns, rows, ch, cols, step_size),
        out_shape=(
            jax.ShapeDtypeStruct((ch, rows, 1, cols), F32),
            jax.ShapeDtypeStruct((ch, rows, 1, cols), F32),
            jax.ShapeDtypeStruct((layers * 9, ch, ch), F32),
        ),
        in_specs=[any_spec, any_spec, any_spec],
        out_specs=(any_spec, any_spec, any_spec),
        scratch_shapes=[
            field(F32), field(F32), field(F32), field(F32), field(F32), field(F32), field(F32),
            vmem((ext + 2, 3 * ch, cols), F32),
            vmem((ext + 2, 3 * ch, cols), F32),
            vmem((ext // 2, 3 * ch, 2 * cols), BF16),
            vmem((ext // 2, 3 * ch, 2 * cols), BF16),
            field(BF16), field(BF16),
            vmem((phases, rows, ch, cols), BF16),
            vmem((phases, nl, ch, cols), BF16),
            vmem((phases, nl, ch, cols), BF16),
            vmem((phases, ext, ch, cols), BF16),
            vmem((layers, 9, ch, ch), BF16),
            vmem((layers, 3 * ch, 3 * ch), BF16),
            vmem((layers, 3 * ch, 3 * ch), BF16),
            vmem((nl, ch, 2 * ch), BF16),
            vmem((nl, ch, 2 * ch), BF16),
            vmem((nl // GROUP, GROUP * ch, 2 * ch), BF16),
            vmem((nl // GROUP, GROUP * ch, 2 * ch), BF16),
            vmem((nl, ch, cols), F32),
            vmem((layers, 3 * ch, 3 * ch), F32),
            vmem((layers, ns, 3 * ch // ns, 3 * ch), F32),
            vmem((layers, 3 * ch, 3 * ch), F32),
            vmem((layers * 9, ch, ch), F32),
            dma((3,)), dma((3,)), dma((2,)), dma((2,)), dma((2,)), dma((2,)),
            dma((nl,)), dma((nl,)),
            dma((nl,)), dma((phases, nl)), dma((nl,)), dma((phases, nl)),
            dma((phases, 4)), dma((phases, 4)),
            dma((layers, ns)), dma((layers, ns)), dma((layers, ns)), dma((layers, ns)),
        ],
        compiler_params=pltpu.CompilerParams(
            collective_id=0, has_side_effects=True, vmem_limit_bytes=56 * 1024 * 1024),
        name="mgrit",
    )(
        image_features.reshape(ch, rows, 1, cols),
        output_cotangent.reshape(ch, rows, 1, cols),
        conv_weights,
    )
    return (
        states.reshape(1, 1, ch, rows, cols),
        starts.reshape(1, 1, ch, rows, cols),
        grads.reshape(layers, 9, ch, ch),
    )


def solution(mesh):
    placed = (
        P(None, None, "space", None),
        P(None, None, "space", None),
        P("layer", None, None, None),
    )
    return jax.shard_map(
        per_device,
        mesh=mesh,
        in_specs=placed,
        out_specs=(
            P("layer", None, None, "space", None),
            P("layer", None, None, "space", None),
            P("layer", None, None, None),
        ),
        check_vma=False,
    )
```

```python
import functools

import jax
import jax.numpy as jnp
from jax import lax
from jax.experimental import pallas as pl
from jax.experimental.pallas import tpu as pltpu
from jax.sharding import PartitionSpec as P

ITERS = 2
HORIZON = 4.0
HALO = 4
GROUP = 4
MESH = pl.DeviceIdType.MESH
F32 = jnp.float32
BF16 = jnp.bfloat16


def kernel(
    nl, ns, rows, ch, cols, step_size,
    u_in, c_in, w_in,
    states_out, adj_out, grads_out,
    u, s, c, a, a1, t0, t1, y0, y1, x0, x1, d0, d1,
    sendq, recvq, sendx, recvx, w, wf, wb, mb, rev_m, fwd_p, rev_p, ys,
    grad, grecv, gsum, gout,
    in_sem, out_sem, uh_send, uh_recv, ch_send, ch_recv,
    b_send, b_recv, q_send, q_recv, x_send, x_recv, h_send, h_recv,
    g_send, g_recv, r_send, r_recv,
):
    me = lax.axis_index("layer")
    space = lax.axis_index("space")
    ext = rows + 2 * HALO
    pairs = ext // 2
    own = rows // 2
    groups = nl // GROUP
    spread_by = nl // 4
    my_row = lax.rem(me, spread_by) * 4 + lax.div(me, spread_by)
    has_up = space > 0
    has_down = space < ns - 1

    def loop(lo, hi, body):
        def step(i, carry):
            body(i)
            return carry
        lax.fori_loop(lo, hi, step, 0)

    def partner(i):
        return lax.rem(me + i, nl)

    def neighbour(i):
        return lax.rem(space + i, ns)

    def scanner(r):
        return lax.rem(r, 4) * spread_by + lax.div(r, 4)

    barrier = pltpu.get_barrier_semaphore()

    def greet(i):
        pl.semaphore_signal(barrier, inc=1, device_id={"layer": partner(i)}, device_id_type=MESH)
    loop(1, nl, greet)

    def greet_space(i):
        pl.semaphore_signal(barrier, inc=1, device_id={"space": neighbour(i)}, device_id_type=MESH)
    loop(1, ns, greet_space)

    in_w = pltpu.make_async_copy(w_in, w, in_sem.at[2])
    in_w.start()
    for r in range(rows):
        pltpu.make_async_copy(u_in.at[:, r, 0], u.at[HALO + r], in_sem.at[0]).start()
    for r in range(rows):
        pltpu.make_async_copy(c_in.at[:, r, 0], c.at[HALO + r], in_sem.at[1]).start()

    def own_rows(ref):
        return ref.at[pl.ds(HALO, rows)]

    blank = jnp.zeros((HALO, ch, cols), F32)
    blank16 = jnp.zeros((HALO, ch, cols), BF16)

    def clear(part):
        for ref in (u, c):
            ref[part] = blank
        for ph in range(2 * ITERS):
            recvx[ph, part] = blank16

    pl.when(space == 0)(lambda: clear(pl.ds(0, HALO)))
    pl.when(space == ns - 1)(lambda: clear(pl.ds(HALO + rows, HALO)))
    for part in (pl.ds(0, HALO - 2), pl.ds(HALO + rows + 2, HALO - 2)):
        c[part] = blank[:HALO - 2]

    for ref in (y0, y1):
        for e in (0, 1, 2, ext - 1, ext, ext + 1):
            ref[e] = jnp.zeros((3 * ch, cols), F32)

    def halves(matrix):
        high = matrix.astype(BF16)
        low = (matrix - high.astype(F32)).astype(BF16)
        return jnp.concatenate([high, low], axis=1)

    in_w.wait()
    summed = w[0, 0].astype(F32)
    for tap in range(1, 9):
        summed = summed + w[0, tap].astype(F32)
    mb[me] = halves(2 * step_size * summed)
    for layer in range(2):
        for ty in range(3):
            wf[layer, ty * ch:(ty + 1) * ch] = jnp.concatenate(
                [w[layer, 3 * ty + tx] for tx in range(3)], axis=1)

    pltpu.make_async_copy(own_rows(u), own_rows(u), in_sem.at[0]).wait()
    pl.semaphore_wait(barrier, nl - 1 + ns - 1)

    def b_copy(i, source):
        k = partner(i)
        return pltpu.make_async_remote_copy(
            src_ref=mb.at[source], dst_ref=mb.at[source], send_sem=b_send.at[k],
            recv_sem=b_recv.at[source], device_id={"layer": k}, device_id_type=MESH)

    up_device = {"space": lax.rem(space + ns - 1, ns)}
    down_device = {"space": lax.rem(space + 1, ns)}

    def edge_copies(ref, width, send, recv):
        up = pltpu.make_async_remote_copy(
            src_ref=ref.at[pl.ds(HALO, width)], dst_ref=ref.at[pl.ds(HALO + rows, width)],
            send_sem=send.at[0], recv_sem=recv.at[1], device_id=up_device, device_id_type=MESH)
        down = pltpu.make_async_remote_copy(
            src_ref=ref.at[pl.ds(HALO + rows - width, width)],
            dst_ref=ref.at[pl.ds(HALO - width, width)],
            send_sem=send.at[1], recv_sem=recv.at[0], device_id=down_device, device_id_type=MESH)
        return up, down

    def edge_start(copies):
        up, down = copies
        pl.when(has_up)(up.start)
        pl.when(has_down)(down.start)

    def edge_wait(copies):
        up, down = copies

        @pl.when(has_up)
        def _():
            up.wait_send()
            down.wait_recv()

        @pl.when(has_down)
        def _():
            down.wait_send()
            up.wait_recv()

    far_u = (
        pltpu.make_async_remote_copy(
            src_ref=u.at[pl.ds(HALO + 2, 2)], dst_ref=u.at[pl.ds(HALO + rows + 2, 2)],
            send_sem=uh_send.at[2], recv_sem=uh_recv.at[3], device_id=up_device,
            device_id_type=MESH),
        pltpu.make_async_remote_copy(
            src_ref=u.at[pl.ds(HALO + rows - 4, 2)], dst_ref=u.at[pl.ds(0, 2)],
            send_sem=uh_send.at[3], recv_sem=uh_recv.at[2], device_id=down_device,
            device_id_type=MESH))
    edge_start(edge_copies(u, 2, uh_send, uh_recv))

    def send_b(i):
        b_copy(i, me).start()
    loop(1, nl, send_b)
    edge_start(far_u)

    lane = lax.broadcasted_iota(jnp.int32, (ch, cols), 1)
    not_first = lane > 0
    not_last = lane < cols - 1

    def shifted(v):
        left = jnp.where(not_first, pltpu.roll(v, 1, 1), 0.0)
        right = jnp.where(not_last, pltpu.roll(v, cols - 1, 1), 0.0)
        return jnp.concatenate([left.astype(BF16), v.astype(BF16), right.astype(BF16)], axis=0)

    def inside(e):
        return jnp.logical_and(
            jnp.logical_or(e >= HALO, has_up), jnp.logical_or(e < HALO + rows, has_down))

    def convolve(which, value, weight, y, keep=None):
        matrix = weight[...]
        values = [(value(2 * p), value(2 * p + 1)) for p in which]
        stacked = [
            jnp.concatenate([shifted(low), shifted(high)], axis=1) for low, high in values]
        products = [jnp.dot(matrix, x, preferred_element_type=F32) for x in stacked]
        for p, x, product in zip(which, stacked, products):
            if keep is not None:
                keep[p] = x
            y[2 * p + 1] = product[:, :cols]
            y[2 * p + 2] = product[:, cols:]

    def gathered(y, e):
        return y[e, 0:ch] + y[e + 1, ch:2 * ch] + y[e + 2, 2 * ch:3 * ch]

    def q_copy(ph, r, source):
        return pltpu.make_async_remote_copy(
            src_ref=sendq.at[ph, r], dst_ref=recvq.at[ph, source],
            send_sem=q_send.at[r], recv_sem=q_recv.at[ph, source],
            device_id={"layer": scanner(r)}, device_id_type=MESH)

    def give_q(ph, which, value):
        for p in which:
            for e in (2 * p, 2 * p + 1):
                r = e - HALO
                entry = value(e)
                if ph % ITERS:
                    entry = entry - sendq[ph - 1, r].astype(F32)
                sendq[ph, r] = entry.astype(BF16)
        for p in which:
            for r in (2 * p - HALO, 2 * p + 1 - HALO):
                pl.when(r != my_row)(lambda r=r: q_copy(ph, r, me).start())

    def wait_q_sent(ph):
        def one(i):
            pl.when(i != my_row)(lambda: q_copy(ph, i, me).wait_send())
        loop(0, rows, one)

    def x_copy(ph, k, row):
        return pltpu.make_async_remote_copy(
            src_ref=sendx.at[ph, k], dst_ref=recvx.at[ph, HALO + row],
            send_sem=x_send.at[k], recv_sem=x_recv.at[ph, row],
            device_id={"layer": k}, device_id_type=MESH)

    def wait_x_sent(ph):
        def one(i):
            x_copy(ph, partner(i), my_row).wait_send()
        loop(1, nl, one)

    def halo_copies(ph, far):
        def one(index, source, target, device):
            return pltpu.make_async_remote_copy(
                src_ref=recvx.at[ph, pl.ds(source, 2)], dst_ref=recvx.at[ph, pl.ds(target, 2)],
                send_sem=h_send.at[ph, index], recv_sem=h_recv.at[ph, index],
                device_id=device, device_id_type=MESH)
        last = HALO + rows
        up = [(0, one(0, HALO, last, up_device))]
        down = [(own - 1, one(2, last - 2, HALO - 2, down_device))]
        if far:
            up.append((1, one(1, HALO + 2, last + 2, up_device)))
            down.append((own - 2, one(3, last - 4, HALO - 4, down_device)))
        return up, down

    inner = max(own - 4, 0)
    first_own = HALO // 2

    def sweep(arrival, far, edge, first_value, first_weight, second_value, second_weight,
              finish, keeps=(None, None), spread=False, last=None):
        def begin(m):
            block = lax.rem(lax.div(me, GROUP) + groups - m, groups)
            places = [2 * block, 2 * block + 1]
            if arrival is not None:
                up, down = halo_copies(arrival, far)
                for place in places:
                    for row in (2 * place, 2 * place + 1):
                        pl.when(row != my_row)(
                            lambda row=row: x_copy(arrival, row, row).wait_recv())
                    for at, copy in up:
                        pl.when(jnp.logical_and(place == at, has_up))(copy.start)
                    for at, copy in down:
                        pl.when(jnp.logical_and(place == at, has_down))(copy.start)
            convolve([first_own + place for place in places],
                     first_value, first_weight, y0, keeps[0])
        loop(0, own // 2, begin)

        def settle():
            if arrival is None:
                edge_wait(edge)
                return
            up, down = halo_copies(arrival, far)

            @pl.when(has_up)
            def _():
                for at, copy in up:
                    copy.wait_send()
                for at, copy in down:
                    copy.wait_recv()

            @pl.when(has_down)
            def _():
                for at, copy in down:
                    copy.wait_send()
                for at, copy in up:
                    copy.wait_recv()

        def rim():
            if spread:
                convolve([0, 1, pairs - 2, pairs - 1], first_value, first_weight, y0, keeps[0])
                return
            convolve([1, pairs - 2], first_value, first_weight, y0, keeps[0])
            if far:
                for e in (0, 1, ext - 2, ext - 1):
                    first_value(e)

        if last is not None:
            last(settle, rim)
            return

        def ring(n):
            start = lax.div(lax.div(me, 2) * inner, own)
            return first_own + 2 + lax.rem(start + inner - 1 + n, inner)

        def second(which):
            convolve(which, second_value, second_weight, y1, keeps[1])

        second([first_own + 1, pairs - first_own - 2])
        if inner:
            second([ring(0), ring(1)])
            second([ring(2), ring(3)])

            def more(m):
                finish([ring(2 * m - 3), ring(2 * m - 2)])
                second([ring(2 * m), ring(2 * m + 1)])
            loop(2, inner // 2, more)
            finish([ring(inner - 3), ring(inner - 2)])
            finish([ring(inner - 1), ring(0)])
        settle()
        rim()
        if spread:
            second([0, 1, 2])
            second([pairs - 3, pairs - 2, pairs - 1])
            finish([1, pairs - 2])
        else:
            second([1, 2, pairs - 3, pairs - 2])
        finish([2, 3])
        finish([pairs - 4, pairs - 3])

    def mixed(matrices, state):
        high = state.astype(BF16)
        low = (state - high.astype(F32)).astype(BF16)
        return jnp.dot(
            jnp.concatenate([matrices, matrices], axis=1),
            jnp.concatenate([high, high, low, low], axis=0), preferred_element_type=F32)

    def prepare(matrices, products):
        total = [None] * groups
        for k in range(GROUP):
            for g in range(groups):
                matrix = matrices[GROUP * g + k]
                plain = matrix[:, :ch].astype(F32) + matrix[:, ch:].astype(F32)
                if k == 0:
                    total[g] = plain
                else:
                    total[g] = total[g] + plain + mixed(matrix, total[g])
                products[g, pl.ds(k * ch, ch)] = halves(total[g])
        for level in range(2):
            reach = 1 << level
            before = list(total)
            for g in range(2 * reach, groups - 1):
                matrix = halves(before[g])
                total[g] = before[g] + before[g - reach] + mixed(matrix, before[g - reach])
                products[g, pl.ds((GROUP + level) * ch, ch)] = halves(total[g])

    def scan(ph, matrices, products, reverse):
        def section(i):
            return nl - 1 - i if reverse else i

        def shift(i):
            j = section(i)
            value = recvq[ph, j].astype(F32)
            if ph % ITERS:
                following = section(min(i + 1, nl - 1))
                value = (value + recvq[ph - 1, j].astype(F32)
                         + sendx[ph - 1, j].astype(F32) - sendx[ph - 1, following].astype(F32))
            return value

        def arrive(j):
            pl.when(j != me)(lambda: q_copy(ph, my_row, j).wait_recv())
        loop(0, nl, arrive)

        state = [None] * groups
        for k in range(GROUP):
            for g in range(groups):
                i = GROUP * g + k
                value = shift(i)
                if k > 0:
                    value = value + state[g] + mixed(matrices[i], state[g])
                state[g] = value
                ys[i] = value

        reach = 1
        level = 0
        while reach < groups - 1:
            before = list(state)
            at = pl.ds((GROUP - 1 + level) * ch, ch)
            for g in range(reach, groups - 1):
                state[g] = before[g] + before[g - reach] + mixed(products[g, at], before[g - reach])
            reach *= 2
            level += 1
        for g in range(1, groups):
            ys[GROUP * g + GROUP - 1] = state[g - 1]
        ys[GROUP - 1] = jnp.zeros((ch, cols), F32)

        def spread_group(n):
            targets = []
            for t in range(2):
                g = lax.rem(lax.div(my_row, GROUP) + 2 * n + t, groups)
                if reverse:
                    g = groups - 1 - g
                start = ys[GROUP * g + GROUP - 1]
                change = mixed(products[g, pl.ds(0, (GROUP - 1) * ch)], start)
                results = [start]
                for k in range(GROUP - 1):
                    results.append(ys[GROUP * g + k] + start + change[k * ch:(k + 1) * ch])
                for k in range(GROUP):
                    j = section(GROUP * g + k)
                    sendx[ph, j] = results[k].astype(BF16)
                    targets.append(j)
            for j in targets:
                pl.when(j != me)(lambda j=j: x_copy(ph, j, my_row).start())
        loop(0, groups // 2, spread_group)
        recvx[ph, HALO + my_row] = sendx[ph, me]

    c_edge = edge_copies(c, 2, ch_send, ch_recv)

    def forward_first(ph, before):
        def value(e):
            if ph is None:
                return u[e]
            new = before[e] + recvx[ph, e].astype(F32)
            s[e] = new
            return new
        return value

    def forward_second(state):
        def value(e):
            tangent = jnp.tanh(gathered(y0, e))
            t0[e] = tangent
            return jnp.where(inside(e), state[e] + step_size * tangent, 0.0)
        return value

    def finish_forward(ph):
        def value(e):
            return step_size * (t0[e] + jnp.tanh(gathered(y1, e)))
        return lambda which: give_q(ph, which, value)

    sweep(None, False, edge_copies(u, 2, uh_send, uh_recv), forward_first(None, None),
          wf.at[0], forward_second(u), wf.at[1], finish_forward(0))
    recvq[0, me] = sendq[0, my_row]

    pltpu.make_async_copy(own_rows(c), own_rows(c), in_sem.at[1]).wait()
    edge_start(c_edge)

    def settle_b(i):
        b_copy(i, me).wait_send()
        b_copy(i, partner(i)).wait_recv()
    loop(1, nl, settle_b)
    prepare(mb, fwd_p)
    edge_wait(far_u)
    scan(0, mb, fwd_p, False)
    wait_q_sent(0)

    sweep(0, True, None, forward_first(0, u), wf.at[0], forward_second(s), wf.at[1],
          finish_forward(1))
    recvq[1, me] = sendq[1, my_row]
    wait_x_sent(0)

    for layer in range(2):
        for ty in range(3):
            wb[layer, ty * ch:(ty + 1) * ch] = jnp.concatenate(
                [w[layer, 8 - 3 * ty - tx].astype(F32).T for tx in range(3)], axis=1).astype(BF16)

    def transpose_b(m):
        for i in range(4):
            matrix = mb[nl - 1 - 4 * m - i].astype(F32).T
            rev_m[4 * m + i] = jnp.concatenate([matrix[:ch], matrix[ch:]], axis=1).astype(BF16)
    loop(0, nl // 4, transpose_b)
    prepare(rev_m, rev_p)
    scan(1, mb, fwd_p, False)
    wait_q_sent(1)

    def finish_last(which):
        for p in which:
            for e in (2 * p, 2 * p + 1):
                t1[e] = jnp.tanh(gathered(y1, e))
    sweep(1, True, None, forward_first(1, s), wf.at[0], forward_second(s), wf.at[1],
          finish_last, keeps=(x0, x1), spread=True)
    wait_x_sent(1)
    for r in range(rows):
        pltpu.make_async_copy(s.at[HALO + r], states_out.at[:, r, 0], out_sem.at[0]).start()

    def scaled(tangent, value):
        return step_size * (1.0 - tangent * tangent) * value

    def adjoint_first(ph, before, keep):
        def value(e):
            if ph is None:
                new = c[e]
            else:
                new = before[e] + recvx[ph, e].astype(F32)
                a[e] = new
            new = scaled(t1[e], new)
            if keep:
                d1[e] = new.astype(BF16)
            return new
        return value

    def adjoint_second(state):
        def value(e):
            after = state[e] + gathered(y0, e)
            return jnp.where(inside(e), scaled(t0[e], after), 0.0)
        return value

    def finish_adjoint(ph):
        def value(e):
            return gathered(y0, e) + gathered(y1, e)
        return lambda which: give_q(ph, which, value)

    sweep(None, False, c_edge, adjoint_first(None, None, False), wb.at[1],
          adjoint_second(c), wb.at[0], finish_adjoint(2))
    recvq[2, me] = sendq[2, my_row]
    scan(2, rev_m, rev_p, True)
    wait_q_sent(2)
    sweep(2, False, None, adjoint_first(2, c, False), wb.at[1],
          adjoint_second(a), wb.at[0], finish_adjoint(3))
    recvq[3, me] = sendq[3, my_row]
    wait_x_sent(2)
    scan(3, rev_m, rev_p, True)
    wait_q_sent(3)

    quarter = 3 * ch // ns

    def gradient(layer, d, x):
        d[pl.ds(0, HALO)] = blank16
        d[pl.ds(HALO + rows, HALO)] = blank16

        many = 3 if (pairs - 2) % 3 == 0 else 2

        def one(m, total):
            which = [1 + many * m + k for k in range(many)]
            left, right = [], []
            for p in which:
                for e in (2 * p, 2 * p + 1):
                    left.append(jnp.concatenate([d[e + 1], d[e], d[e - 1]], axis=0))
                right.append(x[p])
            return total + lax.dot_general(
                jnp.concatenate(left, axis=1), jnp.concatenate(right, axis=1),
                (((1,), (1,)), ((), ())), preferred_element_type=F32)
        grad[layer] = lax.fori_loop(
            0, (pairs - 2) // many, one, jnp.zeros((3 * ch, 3 * ch), F32))
        for i in range(1, ns):
            g_copy(layer, i, space).start()

    def part(index):
        return pl.ds(pl.multiple_of(index * quarter, quarter), quarter)

    def g_copy(layer, i, source):
        k = neighbour(i)
        return pltpu.make_async_remote_copy(
            src_ref=grad.at[layer, part(k)], dst_ref=grecv.at[layer, source],
            send_sem=g_send.at[layer, k], recv_sem=g_recv.at[layer, source],
            device_id={"space": k}, device_id_type=MESH)

    def r_copy(layer, i, source):
        k = neighbour(i)
        return pltpu.make_async_remote_copy(
            src_ref=gsum.at[layer, part(source)], dst_ref=gsum.at[layer, part(source)],
            send_sem=r_send.at[layer, k], recv_sem=r_recv.at[layer, source],
            device_id={"space": k}, device_id_type=MESH)

    def reduce_part(layer):
        total = grad[layer, part(space)]
        for i in range(1, ns):
            g_copy(layer, i, neighbour(i)).wait_recv()
            total = total + grecv[layer, neighbour(i)]
        gsum[layer, part(space)] = total
        for i in range(1, ns):
            r_copy(layer, i, space).start()

    def collect(layer):
        for i in range(1, ns):
            g_copy(layer, i, space).wait_send()
            r_copy(layer, i, neighbour(i)).wait_recv()
            r_copy(layer, i, space).wait_send()
        for ty in range(3):
            for tx in range(3):
                gout[9 * layer + 3 * ty + tx] = (
                    gsum[layer, ty * ch:(ty + 1) * ch, tx * ch:(tx + 1) * ch])

    def last_steps(settle, rim):
        gradient(1, d1, x1)
        settle()
        rim()

        def scale(p):
            for e in (2 * p, 2 * p + 1):
                after = a[e] + gathered(y0, e)
                a1[e] = after
                d0[e] = jnp.where(inside(e), scaled(t0[e], after), 0.0).astype(BF16)

        def scale_two(m):
            scale(1 + 2 * m)
            scale(2 + 2 * m)
        loop(0, (pairs - 2) // 2, scale_two)
        top, bottom = d0[HALO - 1], d0[HALO + rows]
        gradient(0, d0, x0)
        d0[HALO - 1] = top
        d0[HALO + rows] = bottom

        def second(m):
            convolve([1 + 2 * m, 2 + 2 * m], lambda e: d0[e].astype(F32), wb.at[0], y1)
        loop(0, (pairs - 2) // 2, second)

        def end(m):
            for e in range(4):
                at = HALO + 4 * m + e
                a1[at] = a1[at] + gathered(y1, at)
        loop(0, rows // 4, end)

    sweep(3, False, None, adjoint_first(3, a, True), wb.at[1], None, None, None, last=last_steps)
    for r in range(rows):
        pltpu.make_async_copy(a1.at[HALO + r], adj_out.at[:, r, 0], out_sem.at[1]).start()
    wait_x_sent(3)
    reduce_part(1)
    reduce_part(0)
    collect(1)
    collect(0)
    grads = pltpu.make_async_copy(gout, grads_out, out_sem.at[2])
    grads.start()
    pltpu.make_async_copy(own_rows(s), own_rows(s), out_sem.at[0]).wait()
    pltpu.make_async_copy(own_rows(a1), own_rows(a1), out_sem.at[1]).wait()
    grads.wait()


def publish_body(*refs):
    half = len(refs) // 2
    for source, target in zip(refs[:half], refs[half:]):
        target[...] = source[...]


def publish(*arrays):
    steps = 2
    specs = [
        pl.BlockSpec((x.shape[0] // steps,) + x.shape[1:], lambda i, n=x.ndim: (i,) + (0,) * (n - 1))
        for x in arrays]
    return pl.pallas_call(
        publish_body,
        grid=(steps,),
        out_shape=tuple(jax.ShapeDtypeStruct(x.shape, x.dtype) for x in arrays),
        in_specs=specs,
        out_specs=tuple(specs),
        name="publish",
    )(*arrays)


def per_device(image_features, output_cotangent, conv_weights):
    nl, ns = lax.axis_size("layer"), lax.axis_size("space")
    layers, _, ch, _ = conv_weights.shape
    _, _, rows, cols = image_features.shape
    assert rows == nl and layers == 2 and cols == 2 * ch
    step_size = HORIZON / (layers * nl)
    ext = rows + 2 * HALO
    vmem = pltpu.VMEM

    def field(kind):
        return vmem((ext, ch, cols), kind)
    any_spec = pl.BlockSpec(memory_space=pl.ANY)
    dma = pltpu.SemaphoreType.DMA
    phases = 2 * ITERS
    states, starts, grads = pl.pallas_call(
        functools.partial(kernel, nl, ns, rows, ch, cols, step_size),
        out_shape=(
            jax.ShapeDtypeStruct((ch, rows, 1, cols), F32),
            jax.ShapeDtypeStruct((ch, rows, 1, cols), F32),
            jax.ShapeDtypeStruct((layers * 9, ch, ch), F32),
        ),
        in_specs=[any_spec, any_spec, any_spec],
        out_specs=(any_spec, any_spec, any_spec),
        scratch_shapes=[
            field(F32), field(F32), field(F32), field(F32), field(F32), field(F32), field(F32),
            vmem((ext + 2, 3 * ch, cols), F32),
            vmem((ext + 2, 3 * ch, cols), F32),
            vmem((ext // 2, 3 * ch, 2 * cols), BF16),
            vmem((ext // 2, 3 * ch, 2 * cols), BF16),
            field(BF16), field(BF16),
            vmem((phases, rows, ch, cols), BF16),
            vmem((phases, nl, ch, cols), BF16),
            vmem((phases, nl, ch, cols), BF16),
            vmem((phases, ext, ch, cols), BF16),
            vmem((layers, 9, ch, ch), BF16),
            vmem((layers, 3 * ch, 3 * ch), BF16),
            vmem((layers, 3 * ch, 3 * ch), BF16),
            vmem((nl, ch, 2 * ch), BF16),
            vmem((nl, ch, 2 * ch), BF16),
            vmem((nl // GROUP, (GROUP + 2) * ch, 2 * ch), BF16),
            vmem((nl // GROUP, (GROUP + 2) * ch, 2 * ch), BF16),
            vmem((nl, ch, cols), F32),
            vmem((layers, 3 * ch, 3 * ch), F32),
            vmem((layers, ns, 3 * ch // ns, 3 * ch), F32),
            vmem((layers, 3 * ch, 3 * ch), F32),
            vmem((layers * 9, ch, ch), F32),
            dma((3,)), dma((3,)), dma((4,)), dma((4,)), dma((2,)), dma((2,)),
            dma((nl,)), dma((nl,)),
            dma((nl,)), dma((phases, nl)), dma((nl,)), dma((phases, nl)),
            dma((phases, 4)), dma((phases, 4)),
            dma((layers, ns)), dma((layers, ns)), dma((layers, ns)), dma((layers, ns)),
        ],
        compiler_params=pltpu.CompilerParams(
            collective_id=0, has_side_effects=True, vmem_limit_bytes=56 * 1024 * 1024),
        name="mgrit",
    )(
        image_features.reshape(ch, rows, 1, cols),
        output_cotangent.reshape(ch, rows, 1, cols),
        conv_weights,
    )
    states, starts, grads = publish(states.reshape(ch * rows, cols), starts.reshape(ch * rows, cols), grads)
    return (
        states.reshape(1, 1, ch, rows, cols),
        starts.reshape(1, 1, ch, rows, cols),
        grads.reshape(layers, 9, ch, ch),
    )


def solution(mesh):
    placed = (
        P(None, None, "space", None),
        P(None, None, "space", None),
        P("layer", None, None, None),
    )
    return jax.shard_map(
        per_device,
        mesh=mesh,
        in_specs=placed,
        out_specs=(
            P("layer", None, None, "space", None),
            P("layer", None, None, "space", None),
            P("layer", None, None, None),
        ),
        check_vma=False,
    )
```

```python
import functools

import jax
import jax.numpy as jnp
from jax import lax
from jax.experimental import pallas as pl
from jax.experimental.pallas import tpu as pltpu
from jax.sharding import PartitionSpec as P

ITERS = 2
HORIZON = 4.0
HALO = 4
GROUP = 4
MESH = pl.DeviceIdType.MESH
F32 = jnp.float32
BF16 = jnp.bfloat16


def kernel(
    nl, ns, rows, ch, cols, step_size,
    u_in, c_in, w_in,
    states_out, adj_out, grads_out,
    u, s, c, a, a1, t0, t1, y0, y1, x0, x1, d0, d1,
    sendq, recvq, sendx, recvx, w, wf, wb, mb, rev_m, fwd_p, rev_p, ys,
    grad, grecv, gsum, gout,
    in_sem, out_sem, uh_send, uh_recv, ch_send, ch_recv,
    b_send, b_recv, q_send, q_recv, x_send, x_recv, h_send, h_recv,
    g_send, g_recv, r_send, r_recv,
):
    me = lax.axis_index("layer")
    space = lax.axis_index("space")
    ext = rows + 2 * HALO
    pairs = ext // 2
    own = rows // 2
    groups = nl // GROUP
    spread_by = nl // 4
    my_row = lax.rem(me, spread_by) * 4 + lax.div(me, spread_by)
    plane = lax.div(me, spread_by)
    has_up = space > 0
    has_down = space < ns - 1

    def loop(lo, hi, body):
        def step(i, carry):
            body(i)
            return carry
        lax.fori_loop(lo, hi, step, 0)

    def partner(i):
        return lax.rem(me + i, nl)

    def neighbour(i):
        return lax.rem(space + i, ns)

    def scanner(r):
        return lax.rem(r, 4) * spread_by + lax.div(r, 4)

    barrier = pltpu.get_barrier_semaphore()

    def greet(i):
        pl.semaphore_signal(barrier, inc=1, device_id={"layer": partner(i)}, device_id_type=MESH)
    loop(1, nl, greet)

    def greet_space(i):
        pl.semaphore_signal(barrier, inc=1, device_id={"space": neighbour(i)}, device_id_type=MESH)
    loop(1, ns, greet_space)

    in_w = pltpu.make_async_copy(w_in, w, in_sem.at[2])
    in_w.start()
    for r in range(rows):
        pltpu.make_async_copy(u_in.at[:, r, 0], u.at[HALO + r], in_sem.at[0]).start()
    for r in range(rows):
        pltpu.make_async_copy(c_in.at[:, r, 0], c.at[HALO + r], in_sem.at[1]).start()

    def own_rows(ref):
        return ref.at[pl.ds(HALO, rows)]

    blank = jnp.zeros((HALO, ch, cols), F32)
    blank16 = jnp.zeros((HALO, ch, cols), BF16)

    def clear(part):
        for ref in (u, c):
            ref[part] = blank
        for ph in range(2 * ITERS):
            recvx[ph, part] = blank16

    pl.when(space == 0)(lambda: clear(pl.ds(0, HALO)))
    pl.when(space == ns - 1)(lambda: clear(pl.ds(HALO + rows, HALO)))
    for part in (pl.ds(0, HALO - 2), pl.ds(HALO + rows + 2, HALO - 2)):
        c[part] = blank[:HALO - 2]

    for ref in (y0, y1):
        for e in (0, 1, 2, ext - 1, ext, ext + 1):
            ref[e] = jnp.zeros((3 * ch, cols), F32)

    def halves(matrix):
        high = matrix.astype(BF16)
        low = (matrix - high.astype(F32)).astype(BF16)
        return jnp.concatenate([high, low], axis=1)

    in_w.wait()
    summed = w[0, 0].astype(F32)
    for tap in range(1, 9):
        summed = summed + w[0, tap].astype(F32)
    mb[me] = halves(2 * step_size * summed)
    for layer in range(2):
        for ty in range(3):
            wf[layer, ty * ch:(ty + 1) * ch] = jnp.concatenate(
                [w[layer, 3 * ty + tx] for tx in range(3)], axis=1)

    pltpu.make_async_copy(own_rows(u), own_rows(u), in_sem.at[0]).wait()
    pl.semaphore_wait(barrier, nl - 1 + ns - 1)

    def b_copy(i, source):
        k = partner(i)
        return pltpu.make_async_remote_copy(
            src_ref=mb.at[source], dst_ref=mb.at[source], send_sem=b_send.at[k],
            recv_sem=b_recv.at[source], device_id={"layer": k}, device_id_type=MESH)

    up_device = {"space": lax.rem(space + ns - 1, ns)}
    down_device = {"space": lax.rem(space + 1, ns)}

    def edge_copies(ref, width, send, recv):
        up = pltpu.make_async_remote_copy(
            src_ref=ref.at[pl.ds(HALO, width)], dst_ref=ref.at[pl.ds(HALO + rows, width)],
            send_sem=send.at[0], recv_sem=recv.at[1], device_id=up_device, device_id_type=MESH)
        down = pltpu.make_async_remote_copy(
            src_ref=ref.at[pl.ds(HALO + rows - width, width)],
            dst_ref=ref.at[pl.ds(HALO - width, width)],
            send_sem=send.at[1], recv_sem=recv.at[0], device_id=down_device, device_id_type=MESH)
        return up, down

    def edge_start(copies):
        up, down = copies
        pl.when(has_up)(up.start)
        pl.when(has_down)(down.start)

    def edge_wait(copies):
        up, down = copies

        @pl.when(has_up)
        def _():
            up.wait_send()
            down.wait_recv()

        @pl.when(has_down)
        def _():
            down.wait_send()
            up.wait_recv()

    far_u = (
        pltpu.make_async_remote_copy(
            src_ref=u.at[pl.ds(HALO + 2, 2)], dst_ref=u.at[pl.ds(HALO + rows + 2, 2)],
            send_sem=uh_send.at[2], recv_sem=uh_recv.at[3], device_id=up_device,
            device_id_type=MESH),
        pltpu.make_async_remote_copy(
            src_ref=u.at[pl.ds(HALO + rows - 4, 2)], dst_ref=u.at[pl.ds(0, 2)],
            send_sem=uh_send.at[3], recv_sem=uh_recv.at[2], device_id=down_device,
            device_id_type=MESH))
    edge_start(edge_copies(u, 2, uh_send, uh_recv))

    def send_b(i):
        b_copy(i, me).start()
    loop(1, nl, send_b)
    edge_start(far_u)

    lane = lax.broadcasted_iota(jnp.int32, (ch, cols), 1)
    not_first = lane > 0
    not_last = lane < cols - 1

    def shifted(v):
        v = v.astype(BF16)
        nothing = jnp.zeros_like(v)
        left = jnp.where(not_first, pltpu.roll(v, 1, 1), nothing)
        right = jnp.where(not_last, pltpu.roll(v, cols - 1, 1), nothing)
        return jnp.concatenate([left, v, right], axis=0)

    def inside(e):
        return jnp.logical_and(
            jnp.logical_or(e >= HALO, has_up), jnp.logical_or(e < HALO + rows, has_down))

    def convolve(which, value, weight, y, keep=None):
        matrix = weight[...]
        values = [(value(2 * p), value(2 * p + 1)) for p in which]
        stacked = [
            jnp.concatenate([shifted(low), shifted(high)], axis=1) for low, high in values]
        products = [jnp.dot(matrix, x, preferred_element_type=F32) for x in stacked]
        for p, x, product in zip(which, stacked, products):
            if keep is not None:
                keep[p] = x
            y[2 * p + 1] = product[:, :cols]
            y[2 * p + 2] = product[:, cols:]

    def gathered(y, e):
        return y[e, 0:ch] + y[e + 1, ch:2 * ch] + y[e + 2, 2 * ch:3 * ch]

    def q_copy(ph, r, source):
        return pltpu.make_async_remote_copy(
            src_ref=sendq.at[ph, r], dst_ref=recvq.at[ph, source],
            send_sem=q_send.at[r], recv_sem=q_recv.at[ph, source],
            device_id={"layer": scanner(r)}, device_id_type=MESH)

    def give_q(ph, which, value):
        for p in which:
            for e in (2 * p, 2 * p + 1):
                r = e - HALO
                entry = value(e)
                if ph % ITERS:
                    entry = entry - sendq[ph - 1, r].astype(F32)
                sendq[ph, r] = entry.astype(BF16)

        def send():
            for p in which:
                for r in (2 * p - HALO, 2 * p + 1 - HALO):
                    pl.when(r != my_row)(lambda r=r: q_copy(ph, r, me).start())
        return send

    def wait_q_sent(ph):
        def one(i):
            pl.when(i != my_row)(lambda: q_copy(ph, i, me).wait_send())
        loop(0, rows, one)

    def x_copy(ph, k, row):
        return pltpu.make_async_remote_copy(
            src_ref=sendx.at[ph, k], dst_ref=recvx.at[ph, HALO + row],
            send_sem=x_send.at[k], recv_sem=x_recv.at[ph, row],
            device_id={"layer": k}, device_id_type=MESH)

    def wait_x_sent(ph):
        def one(i):
            x_copy(ph, partner(i), my_row).wait_send()
        loop(1, nl, one)

    def halo_copies(ph, far):
        def one(index, source, target, device):
            return pltpu.make_async_remote_copy(
                src_ref=recvx.at[ph, pl.ds(source, 2)], dst_ref=recvx.at[ph, pl.ds(target, 2)],
                send_sem=h_send.at[ph, index], recv_sem=h_recv.at[ph, index],
                device_id=device, device_id_type=MESH)
        last = HALO + rows
        up = [(0, one(0, HALO, last, up_device))]
        down = [(own - 1, one(2, last - 2, HALO - 2, down_device))]
        if far:
            up.append((1, one(1, HALO + 2, last + 2, up_device)))
            down.append((own - 2, one(3, last - 4, HALO - 4, down_device)))
        return up, down

    inner = max(own - 4, 0)
    first_own = HALO // 2

    def sweep(arrival, far, edge, first_value, first_weight, second_value, second_weight,
              finish, keeps=(None, None), spread=False, last=None):
        def begin(m):
            if arrival is None:
                convolve([first_own + 8 * m + k for k in range(8)],
                         first_value, first_weight, y0, keeps[0])
                return
            places = []
            for k in range(4):
                block = lax.rem(lax.div(me, GROUP) + 2 * groups - 4 * m - k, groups)
                places += [2 * block, 2 * block + 1]
            up, down = halo_copies(arrival, far)
            for place in places:
                for row in (2 * place, 2 * place + 1):
                    pl.when(row != my_row)(
                        lambda row=row: x_copy(arrival, row, row).wait_recv())
                for at, copy in up:
                    pl.when(jnp.logical_and(place == at, has_up))(copy.start)
                for at, copy in down:
                    pl.when(jnp.logical_and(place == at, has_down))(copy.start)
            convolve([first_own + place for place in places],
                     first_value, first_weight, y0, keeps[0])
        loop(0, own // 8, begin)

        def settle():
            if arrival is None:
                edge_wait(edge)
                return
            up, down = halo_copies(arrival, far)

            @pl.when(has_up)
            def _():
                for at, copy in up:
                    copy.wait_send()
                for at, copy in down:
                    copy.wait_recv()

            @pl.when(has_down)
            def _():
                for at, copy in down:
                    copy.wait_send()
                for at, copy in up:
                    copy.wait_recv()

        def rim():
            if spread:
                convolve([0, 1, pairs - 2, pairs - 1], first_value, first_weight, y0, keeps[0])
                return
            convolve([1, pairs - 2], first_value, first_weight, y0, keeps[0])
            if far:
                for e in (0, 1, ext - 2, ext - 1):
                    first_value(e)

        if last is not None:
            last(settle, rim)
            return

        def ring(n):
            start = lax.rem(lax.div(lax.rem(me, spread_by), 2) + 2, spread_by // 2)
            start = lax.div(lax.rem(4 * start + plane, own) * inner, own)
            return first_own + 2 + lax.rem(start + inner - 1 + n, inner)

        def second(which):
            convolve(which, second_value, second_weight, y1, keeps[1])

        def both(done, which):
            send = finish(done)
            if send is not None:
                send()
            if which:
                second(which)

        second([first_own + 1, pairs - first_own - 2])
        if inner:
            q = [ring(n) for n in range(inner)]
            second(q[:4])
            for m in range(1, inner // 4):
                both(q[max(4 * m - 5, 1):4 * m - 1], q[4 * m:4 * m + 4])
            both(q[max(inner - 5, 1):] + q[:1], [])
        settle()
        rim()
        if spread:
            second([0, 1, 2])
            second([pairs - 3, pairs - 2, pairs - 1])
            finish([1, pairs - 2])
        else:
            second([1, 2, pairs - 3, pairs - 2])
        both([2, 3], [])
        both([pairs - 4, pairs - 3], [])

    def mixed(matrices, state):
        high = state.astype(BF16)
        low = (state - high.astype(F32)).astype(BF16)
        return jnp.dot(
            jnp.concatenate([matrices, matrices], axis=1),
            jnp.concatenate([high, high, low, low], axis=0), preferred_element_type=F32)

    def prepare(matrices, products):
        total = [None] * groups
        for k in range(GROUP):
            for g in range(groups):
                matrix = matrices[GROUP * g + k]
                plain = matrix[:, :ch].astype(F32) + matrix[:, ch:].astype(F32)
                if k == 0:
                    total[g] = plain
                else:
                    total[g] = total[g] + plain + mixed(matrix, total[g])
                products[g, pl.ds(k * ch, ch)] = halves(total[g])
        for level in range(2):
            reach = 1 << level
            before = list(total)
            for g in range(2 * reach, groups - 1):
                matrix = halves(before[g])
                total[g] = before[g] + before[g - reach] + mixed(matrix, before[g - reach])
                products[g, pl.ds((GROUP + level) * ch, ch)] = halves(total[g])

    def scan(ph, matrices, products, reverse):
        def section(i):
            return nl - 1 - i if reverse else i

        def shift(i):
            j = section(i)
            value = recvq[ph, j].astype(F32)
            if ph % ITERS:
                following = section(min(i + 1, nl - 1))
                value = (value + recvq[ph - 1, j].astype(F32)
                         + sendx[ph - 1, j].astype(F32) - sendx[ph - 1, following].astype(F32))
            return value

        def arrive(j):
            pl.when(j != me)(lambda: q_copy(ph, my_row, j).wait_recv())
        loop(0, nl, arrive)

        state = [None] * groups
        for k in range(GROUP):
            for g in range(groups):
                i = GROUP * g + k
                value = shift(i)
                if k > 0:
                    value = value + state[g] + mixed(matrices[i], state[g])
                state[g] = value
                ys[i] = value

        reach = 1
        level = 0
        while reach < groups - 1:
            before = list(state)
            at = pl.ds((GROUP - 1 + level) * ch, ch)
            for g in range(reach, groups - 1):
                state[g] = before[g] + before[g - reach] + mixed(products[g, at], before[g - reach])
            reach *= 2
            level += 1
        for g in range(1, groups):
            ys[GROUP * g + GROUP - 1] = state[g - 1]
        ys[GROUP - 1] = jnp.zeros((ch, cols), F32)

        def spread_group(n):
            targets = []
            for t in range(2):
                g = lax.rem(lax.div(my_row, GROUP) + 2 * n + t, groups)
                if reverse:
                    g = groups - 1 - g
                start = ys[GROUP * g + GROUP - 1]
                change = mixed(products[g, pl.ds(0, (GROUP - 1) * ch)], start)
                results = [start]
                for k in range(GROUP - 1):
                    results.append(ys[GROUP * g + k] + start + change[k * ch:(k + 1) * ch])
                for k in range(GROUP):
                    j = section(GROUP * g + k)
                    sendx[ph, j] = results[k].astype(BF16)
                    targets.append(j)
            for j in targets:
                pl.when(j != me)(lambda j=j: x_copy(ph, j, my_row).start())
        loop(0, groups // 2, spread_group)
        recvx[ph, HALO + my_row] = sendx[ph, me]

    c_edge = edge_copies(c, 2, ch_send, ch_recv)

    def forward_first(ph, before):
        def value(e):
            if ph is None:
                return u[e]
            new = before[e] + recvx[ph, e].astype(F32)
            s[e] = new
            return new
        return value

    def forward_second(state):
        def value(e):
            tangent = jnp.tanh(gathered(y0, e))
            t0[e] = tangent
            return jnp.where(inside(e), state[e] + step_size * tangent, 0.0)
        return value

    def finish_forward(ph):
        def value(e):
            return step_size * (t0[e] + jnp.tanh(gathered(y1, e)))
        return lambda which: give_q(ph, which, value)

    sweep(None, False, edge_copies(u, 2, uh_send, uh_recv), forward_first(None, None),
          wf.at[0], forward_second(u), wf.at[1], finish_forward(0))
    recvq[0, me] = sendq[0, my_row]

    pltpu.make_async_copy(own_rows(c), own_rows(c), in_sem.at[1]).wait()
    edge_start(c_edge)

    def settle_b(i):
        b_copy(i, me).wait_send()
        b_copy(i, partner(i)).wait_recv()
    loop(1, nl, settle_b)
    prepare(mb, fwd_p)
    edge_wait(far_u)
    scan(0, mb, fwd_p, False)
    wait_q_sent(0)

    sweep(0, True, None, forward_first(0, u), wf.at[0], forward_second(s), wf.at[1],
          finish_forward(1))
    recvq[1, me] = sendq[1, my_row]
    wait_x_sent(0)

    for layer in range(2):
        for ty in range(3):
            wb[layer, ty * ch:(ty + 1) * ch] = jnp.concatenate(
                [w[layer, 8 - 3 * ty - tx].astype(F32).T for tx in range(3)], axis=1).astype(BF16)

    def transpose_b(m):
        for i in range(4):
            matrix = mb[nl - 1 - 4 * m - i].astype(F32).T
            rev_m[4 * m + i] = jnp.concatenate([matrix[:ch], matrix[ch:]], axis=1).astype(BF16)
    loop(0, nl // 4, transpose_b)
    prepare(rev_m, rev_p)
    scan(1, mb, fwd_p, False)
    wait_q_sent(1)

    def finish_last(which):
        for p in which:
            for e in (2 * p, 2 * p + 1):
                t1[e] = jnp.tanh(gathered(y1, e))
    sweep(1, True, None, forward_first(1, s), wf.at[0], forward_second(s), wf.at[1],
          finish_last, keeps=(x0, x1), spread=True)
    wait_x_sent(1)
    for r in range(rows):
        pltpu.make_async_copy(s.at[HALO + r], states_out.at[:, r, 0], out_sem.at[0]).start()

    def scaled(tangent, value):
        return step_size * (1.0 - tangent * tangent) * value

    def adjoint_first(ph, before, keep):
        def value(e):
            if ph is None:
                new = c[e]
            else:
                new = before[e] + recvx[ph, e].astype(F32)
                a[e] = new
            new = scaled(t1[e], new)
            if keep:
                d1[e] = new.astype(BF16)
            return new
        return value

    def adjoint_second(state):
        def value(e):
            after = state[e] + gathered(y0, e)
            return jnp.where(inside(e), scaled(t0[e], after), 0.0)
        return value

    def finish_adjoint(ph):
        def value(e):
            return gathered(y0, e) + gathered(y1, e)
        return lambda which: give_q(ph, which, value)

    sweep(None, False, c_edge, adjoint_first(None, None, False), wb.at[1],
          adjoint_second(c), wb.at[0], finish_adjoint(2))
    recvq[2, me] = sendq[2, my_row]
    scan(2, rev_m, rev_p, True)
    wait_q_sent(2)
    sweep(2, False, None, adjoint_first(2, c, False), wb.at[1],
          adjoint_second(a), wb.at[0], finish_adjoint(3))
    recvq[3, me] = sendq[3, my_row]
    wait_x_sent(2)
    scan(3, rev_m, rev_p, True)
    wait_q_sent(3)

    quarter = 3 * ch // ns
    many = 3 if (pairs - 2) % 3 == 0 else 2

    def gradient(layer, d, x):
        d[pl.ds(0, HALO)] = blank16
        d[pl.ds(HALO + rows, HALO)] = blank16

        def one(m, total):
            which = [1 + many * m + k for k in range(many)]
            left, right = [], []
            for p in which:
                for e in (2 * p, 2 * p + 1):
                    left.append(jnp.concatenate([d[e + 1], d[e], d[e - 1]], axis=0))
                right.append(x[p])
            return total + lax.dot_general(
                jnp.concatenate(left, axis=1), jnp.concatenate(right, axis=1),
                (((1,), (1,)), ((), ())), preferred_element_type=F32)
        grad[layer] = lax.fori_loop(
            0, (pairs - 2) // many, one, jnp.zeros((3 * ch, 3 * ch), F32))
        for i in range(1, ns):
            g_copy(layer, i, space).start()

    def part(index):
        return pl.ds(pl.multiple_of(index * quarter, quarter), quarter)

    def g_copy(layer, i, source):
        k = neighbour(i)
        return pltpu.make_async_remote_copy(
            src_ref=grad.at[layer, part(k)], dst_ref=grecv.at[layer, source],
            send_sem=g_send.at[layer, k], recv_sem=g_recv.at[layer, source],
            device_id={"space": k}, device_id_type=MESH)

    def r_copy(layer, i, source):
        k = neighbour(i)
        return pltpu.make_async_remote_copy(
            src_ref=gsum.at[layer, part(source)], dst_ref=gsum.at[layer, part(source)],
            send_sem=r_send.at[layer, k], recv_sem=r_recv.at[layer, source],
            device_id={"space": k}, device_id_type=MESH)

    def reduce_part(layer):
        total = grad[layer, part(space)]
        for i in range(1, ns):
            g_copy(layer, i, neighbour(i)).wait_recv()
            total = total + grecv[layer, neighbour(i)]
        gsum[layer, part(space)] = total
        for i in range(1, ns):
            r_copy(layer, i, space).start()

    def collect(layer):
        for i in range(1, ns):
            g_copy(layer, i, space).wait_send()
            r_copy(layer, i, neighbour(i)).wait_recv()
            r_copy(layer, i, space).wait_send()
        for ty in range(3):
            for tx in range(3):
                gout[9 * layer + 3 * ty + tx] = (
                    gsum[layer, ty * ch:(ty + 1) * ch, tx * ch:(tx + 1) * ch])

    def last_steps(settle, rim):
        gradient(1, d1, x1)
        settle()
        rim()

        def scale(p):
            for e in (2 * p, 2 * p + 1):
                after = a[e] + gathered(y0, e)
                a1[e] = after
                d0[e] = jnp.where(inside(e), scaled(t0[e], after), 0.0).astype(BF16)

        def scale_some(m):
            for k in range(many):
                scale(1 + many * m + k)
        loop(0, (pairs - 2) // many, scale_some)
        top, bottom = d0[HALO - 1], d0[HALO + rows]
        gradient(0, d0, x0)
        d0[HALO - 1] = top
        d0[HALO + rows] = bottom

        wait_x_sent(3)
        reduce_part(1)

        def second(m):
            convolve([1 + many * m + k for k in range(many)],
                     lambda e: d0[e].astype(F32), wb.at[0], y1)
        loop(0, (pairs - 2) // many, second)
        reduce_part(0)

        def end(m):
            for e in range(4):
                at = HALO + 4 * m + e
                a1[at] = a1[at] + gathered(y1, at)
        loop(0, rows // 4, end)

    sweep(3, False, None, adjoint_first(3, a, True), wb.at[1], None, None, None, last=last_steps)
    for r in range(rows):
        pltpu.make_async_copy(a1.at[HALO + r], adj_out.at[:, r, 0], out_sem.at[1]).start()
    collect(1)
    collect(0)
    grads = pltpu.make_async_copy(gout, grads_out, out_sem.at[2])
    grads.start()
    pltpu.make_async_copy(own_rows(s), own_rows(s), out_sem.at[0]).wait()
    pltpu.make_async_copy(own_rows(a1), own_rows(a1), out_sem.at[1]).wait()
    grads.wait()


def publish_body(*refs):
    half = len(refs) // 2
    for source, target in zip(refs[:half], refs[half:]):
        target[...] = source[...]


def publish(*arrays):
    steps = 2
    specs = [
        pl.BlockSpec((x.shape[0] // steps,) + x.shape[1:], lambda i, n=x.ndim: (i,) + (0,) * (n - 1))
        for x in arrays]
    return pl.pallas_call(
        publish_body,
        grid=(steps,),
        out_shape=tuple(jax.ShapeDtypeStruct(x.shape, x.dtype) for x in arrays),
        in_specs=specs,
        out_specs=tuple(specs),
        name="publish",
    )(*arrays)


def per_device(image_features, output_cotangent, conv_weights):
    nl, ns = lax.axis_size("layer"), lax.axis_size("space")
    layers, _, ch, _ = conv_weights.shape
    _, _, rows, cols = image_features.shape
    assert rows == nl and layers == 2 and cols == 2 * ch
    step_size = HORIZON / (layers * nl)
    ext = rows + 2 * HALO
    vmem = pltpu.VMEM

    def field(kind):
        return vmem((ext, ch, cols), kind)
    any_spec = pl.BlockSpec(memory_space=pl.ANY)
    dma = pltpu.SemaphoreType.DMA
    phases = 2 * ITERS
    states, starts, grads = pl.pallas_call(
        functools.partial(kernel, nl, ns, rows, ch, cols, step_size),
        out_shape=(
            jax.ShapeDtypeStruct((ch, rows, 1, cols), F32),
            jax.ShapeDtypeStruct((ch, rows, 1, cols), F32),
            jax.ShapeDtypeStruct((layers * 9, ch, ch), F32),
        ),
        in_specs=[any_spec, any_spec, any_spec],
        out_specs=(any_spec, any_spec, any_spec),
        scratch_shapes=[
            field(F32), field(F32), field(F32), field(F32), field(F32), field(F32), field(F32),
            vmem((ext + 2, 3 * ch, cols), F32),
            vmem((ext + 2, 3 * ch, cols), F32),
            vmem((ext // 2, 3 * ch, 2 * cols), BF16),
            vmem((ext // 2, 3 * ch, 2 * cols), BF16),
            field(BF16), field(BF16),
            vmem((phases, rows, ch, cols), BF16),
            vmem((phases, nl, ch, cols), BF16),
            vmem((phases, nl, ch, cols), BF16),
            vmem((phases, ext, ch, cols), BF16),
            vmem((layers, 9, ch, ch), BF16),
            vmem((layers, 3 * ch, 3 * ch), BF16),
            vmem((layers, 3 * ch, 3 * ch), BF16),
            vmem((nl, ch, 2 * ch), BF16),
            vmem((nl, ch, 2 * ch), BF16),
            vmem((nl // GROUP, (GROUP + 2) * ch, 2 * ch), BF16),
            vmem((nl // GROUP, (GROUP + 2) * ch, 2 * ch), BF16),
            vmem((nl, ch, cols), F32),
            vmem((layers, 3 * ch, 3 * ch), F32),
            vmem((layers, ns, 3 * ch // ns, 3 * ch), F32),
            vmem((layers, 3 * ch, 3 * ch), F32),
            vmem((layers * 9, ch, ch), F32),
            dma((3,)), dma((3,)), dma((4,)), dma((4,)), dma((2,)), dma((2,)),
            dma((nl,)), dma((nl,)),
            dma((nl,)), dma((phases, nl)), dma((nl,)), dma((phases, nl)),
            dma((phases, 4)), dma((phases, 4)),
            dma((layers, ns)), dma((layers, ns)), dma((layers, ns)), dma((layers, ns)),
        ],
        compiler_params=pltpu.CompilerParams(
            collective_id=0, has_side_effects=True, vmem_limit_bytes=56 * 1024 * 1024),
        name="mgrit",
    )(
        image_features.reshape(ch, rows, 1, cols),
        output_cotangent.reshape(ch, rows, 1, cols),
        conv_weights,
    )
    states, starts, grads = publish(
        states.reshape(ch * rows, cols), starts.reshape(ch * rows, cols),
        grads.reshape(layers * 9 * ch, ch))
    return (
        states.reshape(1, 1, ch, rows, cols),
        starts.reshape(1, 1, ch, rows, cols),
        grads.reshape(layers, 9, ch, ch),
    )


def solution(mesh):
    placed = (
        P(None, None, "space", None),
        P(None, None, "space", None),
        P("layer", None, None, None),
    )
    return jax.shard_map(
        per_device,
        mesh=mesh,
        in_specs=placed,
        out_specs=(
            P("layer", None, None, "space", None),
            P("layer", None, None, "space", None),
            P("layer", None, None, None),
        ),
        check_vma=False,
    )
```

```python
import functools

import jax
import jax.numpy as jnp
from jax import lax
from jax.experimental import pallas as pl
from jax.experimental.pallas import tpu as pltpu
from jax.sharding import PartitionSpec as P

ITERS = 2
HORIZON = 4.0
HALO = 4
GROUP = 4
MESH = pl.DeviceIdType.MESH
F32 = jnp.float32
BF16 = jnp.bfloat16


def kernel(
    nl, ns, rows, ch, cols, step_size,
    u_in, c_in, w_in,
    states_out, adj_out, grads_out,
    u, s, c, a, a1, t0, t1, y0, y1, x0, x1, d0, d1,
    sendq, recvq, sendx, recvx, w, wf, wb, mb, rev_m, fwd_p, rev_p, ys,
    grad, grecv, gsum, gout,
    in_sem, out_sem, uh_send, uh_recv, ch_send, ch_recv,
    b_send, b_recv, q_send, q_recv, x_send, x_recv, h_send, h_recv,
    g_send, g_recv, r_send, r_recv,
):
    me = lax.axis_index("layer")
    space = lax.axis_index("space")
    ext = rows + 2 * HALO
    pairs = ext // 2
    own = rows // 2
    groups = nl // GROUP
    spread_by = nl // 4
    my_row = lax.rem(me, spread_by) * 4 + lax.div(me, spread_by)
    plane = lax.div(me, spread_by)
    has_up = space > 0
    has_down = space < ns - 1

    def loop(lo, hi, body):
        def step(i, carry):
            body(i)
            return carry
        lax.fori_loop(lo, hi, step, 0)

    def partner(i):
        return lax.rem(me + i, nl)

    def neighbour(i):
        return lax.rem(space + i, ns)

    def scanner(r):
        return lax.rem(r, 4) * spread_by + lax.div(r, 4)

    barrier = pltpu.get_barrier_semaphore()

    def greet(i):
        pl.semaphore_signal(barrier, inc=1, device_id={"layer": partner(i)}, device_id_type=MESH)
    loop(1, nl, greet)

    def greet_space(i):
        pl.semaphore_signal(barrier, inc=1, device_id={"space": neighbour(i)}, device_id_type=MESH)
    loop(1, ns, greet_space)

    in_w = pltpu.make_async_copy(w_in, w, in_sem.at[2])
    in_w.start()
    for r in range(rows):
        pltpu.make_async_copy(u_in.at[:, r, 0], u.at[HALO + r], in_sem.at[0]).start()
    for r in range(rows):
        pltpu.make_async_copy(c_in.at[:, r, 0], c.at[HALO + r], in_sem.at[1]).start()

    def own_rows(ref):
        return ref.at[pl.ds(HALO, rows)]

    blank = jnp.zeros((HALO, ch, cols), F32)
    blank16 = jnp.zeros((HALO, ch, cols), BF16)

    def clear(part):
        for ref in (u, c):
            ref[part] = blank
        for ph in range(2 * ITERS):
            recvx[ph, part] = blank16

    pl.when(space == 0)(lambda: clear(pl.ds(0, HALO)))
    pl.when(space == ns - 1)(lambda: clear(pl.ds(HALO + rows, HALO)))
    for part in (pl.ds(0, HALO - 2), pl.ds(HALO + rows + 2, HALO - 2)):
        c[part] = blank[:HALO - 2]

    for ref in (y0, y1):
        for e in (0, 1, 2, ext - 1, ext, ext + 1):
            ref[e] = jnp.zeros((3 * ch, cols), F32)

    def halves(matrix):
        high = matrix.astype(BF16)
        low = (matrix - high.astype(F32)).astype(BF16)
        return jnp.concatenate([high, low], axis=1)

    in_w.wait()
    summed = w[0, 0].astype(F32)
    for tap in range(1, 9):
        summed = summed + w[0, tap].astype(F32)
    mb[me] = halves(2 * step_size * summed)
    for layer in range(2):
        for ty in range(3):
            wf[layer, ty * ch:(ty + 1) * ch] = jnp.concatenate(
                [w[layer, 3 * ty + tx] for tx in range(3)], axis=1)

    pltpu.make_async_copy(own_rows(u), own_rows(u), in_sem.at[0]).wait()
    pl.semaphore_wait(barrier, nl - 1 + ns - 1)

    def b_copy(i, source):
        k = partner(i)
        return pltpu.make_async_remote_copy(
            src_ref=mb.at[source], dst_ref=mb.at[source], send_sem=b_send.at[k],
            recv_sem=b_recv.at[source], device_id={"layer": k}, device_id_type=MESH)

    up_device = {"space": lax.rem(space + ns - 1, ns)}
    down_device = {"space": lax.rem(space + 1, ns)}

    def edge_copies(ref, width, send, recv):
        up = pltpu.make_async_remote_copy(
            src_ref=ref.at[pl.ds(HALO, width)], dst_ref=ref.at[pl.ds(HALO + rows, width)],
            send_sem=send.at[0], recv_sem=recv.at[1], device_id=up_device, device_id_type=MESH)
        down = pltpu.make_async_remote_copy(
            src_ref=ref.at[pl.ds(HALO + rows - width, width)],
            dst_ref=ref.at[pl.ds(HALO - width, width)],
            send_sem=send.at[1], recv_sem=recv.at[0], device_id=down_device, device_id_type=MESH)
        return up, down

    def edge_start(copies):
        up, down = copies
        pl.when(has_up)(up.start)
        pl.when(has_down)(down.start)

    def edge_wait(copies):
        up, down = copies

        @pl.when(has_up)
        def _():
            up.wait_send()
            down.wait_recv()

        @pl.when(has_down)
        def _():
            down.wait_send()
            up.wait_recv()

    far_u = (
        pltpu.make_async_remote_copy(
            src_ref=u.at[pl.ds(HALO + 2, 2)], dst_ref=u.at[pl.ds(HALO + rows + 2, 2)],
            send_sem=uh_send.at[2], recv_sem=uh_recv.at[3], device_id=up_device,
            device_id_type=MESH),
        pltpu.make_async_remote_copy(
            src_ref=u.at[pl.ds(HALO + rows - 4, 2)], dst_ref=u.at[pl.ds(0, 2)],
            send_sem=uh_send.at[3], recv_sem=uh_recv.at[2], device_id=down_device,
            device_id_type=MESH))
    edge_start(edge_copies(u, 2, uh_send, uh_recv))

    def send_b(i):
        b_copy(i, me).start()
    loop(1, nl, send_b)
    edge_start(far_u)

    lane = lax.broadcasted_iota(jnp.int32, (ch, cols), 1)
    not_first = lane > 0
    not_last = lane < cols - 1

    def shifted(v):
        v = v.astype(BF16)
        nothing = jnp.zeros_like(v)
        left = jnp.where(not_first, pltpu.roll(v, 1, 1), nothing)
        right = jnp.where(not_last, pltpu.roll(v, cols - 1, 1), nothing)
        return jnp.concatenate([left, v, right], axis=0)

    def inside(e):
        return jnp.logical_and(
            jnp.logical_or(e >= HALO, has_up), jnp.logical_or(e < HALO + rows, has_down))

    def convolve(which, value, weight, y, keep=None):
        matrix = weight[...]
        values = [(value(2 * p), value(2 * p + 1)) for p in which]
        stacked = [
            jnp.concatenate([shifted(low), shifted(high)], axis=1) for low, high in values]
        products = [jnp.dot(matrix, x, preferred_element_type=F32) for x in stacked]
        for p, x, product in zip(which, stacked, products):
            if keep is not None:
                keep[p] = x
            y[2 * p + 1] = product[:, :cols]
            y[2 * p + 2] = product[:, cols:]

    def gathered(y, e):
        return y[e, 0:ch] + y[e + 1, ch:2 * ch] + y[e + 2, 2 * ch:3 * ch]

    def q_copy(ph, r, source):
        return pltpu.make_async_remote_copy(
            src_ref=sendq.at[ph, r], dst_ref=recvq.at[ph, source],
            send_sem=q_send.at[r], recv_sem=q_recv.at[ph, source],
            device_id={"layer": scanner(r)}, device_id_type=MESH)

    def give_q(ph, which, value):
        for p in which:
            for e in (2 * p, 2 * p + 1):
                r = e - HALO
                entry = value(e)
                if ph % ITERS:
                    entry = entry - sendq[ph - 1, r].astype(F32)
                sendq[ph, r] = entry.astype(BF16)

        def send():
            for p in which:
                for r in (2 * p - HALO, 2 * p + 1 - HALO):
                    pl.when(r != my_row)(lambda r=r: q_copy(ph, r, me).start())
        return send

    def wait_q_sent(ph):
        def one(i):
            pl.when(i != my_row)(lambda: q_copy(ph, i, me).wait_send())
        loop(0, rows, one)

    def x_copy(ph, k, row):
        return pltpu.make_async_remote_copy(
            src_ref=sendx.at[ph, k], dst_ref=recvx.at[ph, HALO + row],
            send_sem=x_send.at[k], recv_sem=x_recv.at[ph, row],
            device_id={"layer": k}, device_id_type=MESH)

    def wait_x_sent(ph):
        def one(i):
            x_copy(ph, partner(i), my_row).wait_send()
        loop(1, nl, one)

    def halo_copies(ph, far):
        def one(index, source, target, device):
            return pltpu.make_async_remote_copy(
                src_ref=recvx.at[ph, pl.ds(source, 2)], dst_ref=recvx.at[ph, pl.ds(target, 2)],
                send_sem=h_send.at[ph, index], recv_sem=h_recv.at[ph, index],
                device_id=device, device_id_type=MESH)
        last = HALO + rows
        up = [(0, one(0, HALO, last, up_device))]
        down = [(own - 1, one(2, last - 2, HALO - 2, down_device))]
        if far:
            up.append((1, one(1, HALO + 2, last + 2, up_device)))
            down.append((own - 2, one(3, last - 4, HALO - 4, down_device)))
        return up, down

    inner = max(own - 4, 0)
    first_own = HALO // 2

    def sweep(arrival, far, edge, first_value, first_weight, second_value, second_weight,
              finish, keeps=(None, None), spread=False, last=None):
        def begin(m):
            if arrival is None:
                convolve([first_own + 8 * m + k for k in range(8)],
                         first_value, first_weight, y0, keeps[0])
                return
            places = []
            for k in range(4):
                block = lax.rem(lax.div(me, GROUP) + 2 * groups - 4 * m - k, groups)
                places += [2 * block, 2 * block + 1]
            up, down = halo_copies(arrival, far)
            for place in places:
                for row in (2 * place, 2 * place + 1):
                    pl.when(row != my_row)(
                        lambda row=row: x_copy(arrival, row, row).wait_recv())
                for at, copy in up:
                    pl.when(jnp.logical_and(place == at, has_up))(copy.start)
                for at, copy in down:
                    pl.when(jnp.logical_and(place == at, has_down))(copy.start)
            convolve([first_own + place for place in places],
                     first_value, first_weight, y0, keeps[0])
        loop(0, own // 8, begin)

        def settle():
            if arrival is None:
                edge_wait(edge)
                return
            up, down = halo_copies(arrival, far)

            @pl.when(has_up)
            def _():
                for at, copy in up:
                    copy.wait_send()
                for at, copy in down:
                    copy.wait_recv()

            @pl.when(has_down)
            def _():
                for at, copy in down:
                    copy.wait_send()
                for at, copy in up:
                    copy.wait_recv()

        def rim():
            if spread:
                convolve([0, 1, pairs - 2, pairs - 1], first_value, first_weight, y0, keeps[0])
                return
            convolve([1, pairs - 2], first_value, first_weight, y0, keeps[0])
            if far:
                for e in (0, 1, ext - 2, ext - 1):
                    first_value(e)

        if last is not None:
            last(settle, rim)
            return

        def ring(n):
            start = lax.rem(lax.div(lax.rem(me, spread_by), 2) + 2, spread_by // 2)
            start = lax.div(lax.rem(4 * start + plane, own) * inner, own)
            return first_own + 2 + lax.rem(start + inner - 1 + n, inner)

        def second(which):
            convolve(which, second_value, second_weight, y1, keeps[1])

        def both(done, which):
            send = finish(done)
            if send is not None:
                send()
            if which:
                second(which)

        second([first_own + 1, pairs - first_own - 2])
        if inner:
            q = [ring(n) for n in range(inner)]
            second(q[:4])
            for m in range(1, inner // 4):
                both(q[max(4 * m - 5, 1):4 * m - 1], q[4 * m:4 * m + 4])
            both(q[max(inner - 5, 1):] + q[:1], [])
        settle()
        rim()
        if spread:
            second([0, 1, 2])
            second([pairs - 3, pairs - 2, pairs - 1])
            finish([1, pairs - 2])
        else:
            second([1, 2, pairs - 3, pairs - 2])
        both([2, 3], [])
        both([pairs - 4, pairs - 3], [])

    def mixed(matrices, state):
        high = state.astype(BF16)
        low = (state - high.astype(F32)).astype(BF16)
        return jnp.dot(
            jnp.concatenate([matrices, matrices], axis=1),
            jnp.concatenate([high, high, low, low], axis=0), preferred_element_type=F32)

    def prepare(matrices, products):
        total = [None] * groups
        for k in range(GROUP):
            for g in range(groups):
                matrix = matrices[GROUP * g + k]
                plain = matrix[:, :ch].astype(F32) + matrix[:, ch:].astype(F32)
                if k == 0:
                    total[g] = plain
                else:
                    total[g] = total[g] + plain + mixed(matrix, total[g])
                products[g, pl.ds(k * ch, ch)] = halves(total[g])
        for level in range(2):
            reach = 1 << level
            before = list(total)
            for g in range(2 * reach, groups - 1):
                matrix = halves(before[g])
                total[g] = before[g] + before[g - reach] + mixed(matrix, before[g - reach])
                products[g, pl.ds((GROUP + level) * ch, ch)] = halves(total[g])

    def scan(ph, matrices, products, reverse):
        def section(i):
            return nl - 1 - i if reverse else i

        def shift(i):
            j = section(i)
            value = recvq[ph, j].astype(F32)
            if ph % ITERS:
                following = section(min(i + 1, nl - 1))
                value = (value + recvq[ph - 1, j].astype(F32)
                         + sendx[ph - 1, j].astype(F32) - sendx[ph - 1, following].astype(F32))
            return value

        def arrive(j):
            pl.when(j != me)(lambda: q_copy(ph, my_row, j).wait_recv())
        loop(0, nl, arrive)

        state = [None] * groups
        for k in range(GROUP):
            for g in range(groups):
                i = GROUP * g + k
                value = shift(i)
                if k > 0:
                    value = value + state[g] + mixed(matrices[i], state[g])
                state[g] = value
                ys[i] = value

        reach = 1
        level = 0
        while reach < groups - 1:
            before = list(state)
            at = pl.ds((GROUP - 1 + level) * ch, ch)
            for g in range(reach, groups - 1):
                state[g] = before[g] + before[g - reach] + mixed(products[g, at], before[g - reach])
            reach *= 2
            level += 1
        for g in range(1, groups):
            ys[GROUP * g + GROUP - 1] = state[g - 1]
        ys[GROUP - 1] = jnp.zeros((ch, cols), F32)

        def spread_group(n):
            targets = []
            for t in range(4):
                g = lax.rem(lax.div(my_row, GROUP) + 4 * n + t, groups)
                if reverse:
                    g = groups - 1 - g
                start = ys[GROUP * g + GROUP - 1]
                change = mixed(products[g, pl.ds(0, (GROUP - 1) * ch)], start)
                results = [start]
                for k in range(GROUP - 1):
                    results.append(ys[GROUP * g + k] + start + change[k * ch:(k + 1) * ch])
                for k in range(GROUP):
                    j = section(GROUP * g + k)
                    sendx[ph, j] = results[k].astype(BF16)
                    targets.append(j)
            for j in targets:
                pl.when(j != me)(lambda j=j: x_copy(ph, j, my_row).start())
        loop(0, groups // 4, spread_group)
        recvx[ph, HALO + my_row] = sendx[ph, me]

    c_edge = edge_copies(c, 2, ch_send, ch_recv)

    def forward_first(ph, before):
        def value(e):
            if ph is None:
                return u[e]
            new = before[e] + recvx[ph, e].astype(F32)
            s[e] = new
            return new
        return value

    def forward_second(state):
        def value(e):
            tangent = jnp.tanh(gathered(y0, e))
            t0[e] = tangent
            return jnp.where(inside(e), state[e] + step_size * tangent, 0.0)
        return value

    def finish_forward(ph):
        def value(e):
            return step_size * (t0[e] + jnp.tanh(gathered(y1, e)))
        return lambda which: give_q(ph, which, value)

    sweep(None, False, edge_copies(u, 2, uh_send, uh_recv), forward_first(None, None),
          wf.at[0], forward_second(u), wf.at[1], finish_forward(0))
    recvq[0, me] = sendq[0, my_row]

    pltpu.make_async_copy(own_rows(c), own_rows(c), in_sem.at[1]).wait()
    edge_start(c_edge)

    def settle_b(i):
        b_copy(i, me).wait_send()
        b_copy(i, partner(i)).wait_recv()
    loop(1, nl, settle_b)
    prepare(mb, fwd_p)
    edge_wait(far_u)
    scan(0, mb, fwd_p, False)
    wait_q_sent(0)

    sweep(0, True, None, forward_first(0, u), wf.at[0], forward_second(s), wf.at[1],
          finish_forward(1))
    recvq[1, me] = sendq[1, my_row]
    wait_x_sent(0)

    for layer in range(2):
        for ty in range(3):
            wb[layer, ty * ch:(ty + 1) * ch] = jnp.concatenate(
                [w[layer, 8 - 3 * ty - tx].astype(F32).T for tx in range(3)], axis=1).astype(BF16)

    def transpose_b(m):
        for i in range(4):
            matrix = mb[nl - 1 - 4 * m - i].astype(F32).T
            rev_m[4 * m + i] = jnp.concatenate([matrix[:ch], matrix[ch:]], axis=1).astype(BF16)
    loop(0, nl // 4, transpose_b)
    prepare(rev_m, rev_p)
    scan(1, mb, fwd_p, False)
    wait_q_sent(1)

    def finish_last(which):
        for p in which:
            for e in (2 * p, 2 * p + 1):
                t1[e] = jnp.tanh(gathered(y1, e))
    sweep(1, True, None, forward_first(1, s), wf.at[0], forward_second(s), wf.at[1],
          finish_last, keeps=(x0, x1), spread=True)
    wait_x_sent(1)
    for r in range(rows):
        pltpu.make_async_copy(s.at[HALO + r], states_out.at[:, r, 0], out_sem.at[0]).start()

    def scaled(tangent, value):
        return step_size * (1.0 - tangent * tangent) * value

    def adjoint_first(ph, before, keep):
        def value(e):
            if ph is None:
                new = c[e]
            else:
                new = before[e] + recvx[ph, e].astype(F32)
                a[e] = new
            new = scaled(t1[e], new)
            if keep:
                d1[e] = new.astype(BF16)
            return new
        return value

    def adjoint_second(state):
        def value(e):
            after = state[e] + gathered(y0, e)
            return jnp.where(inside(e), scaled(t0[e], after), 0.0)
        return value

    def finish_adjoint(ph):
        def value(e):
            return gathered(y0, e) + gathered(y1, e)
        return lambda which: give_q(ph, which, value)

    sweep(None, False, c_edge, adjoint_first(None, None, False), wb.at[1],
          adjoint_second(c), wb.at[0], finish_adjoint(2))
    recvq[2, me] = sendq[2, my_row]
    scan(2, rev_m, rev_p, True)
    wait_q_sent(2)
    sweep(2, False, None, adjoint_first(2, c, False), wb.at[1],
          adjoint_second(a), wb.at[0], finish_adjoint(3))
    recvq[3, me] = sendq[3, my_row]
    wait_x_sent(2)
    scan(3, rev_m, rev_p, True)
    wait_q_sent(3)

    quarter = 3 * ch // ns
    many = 6 if (pairs - 2) % 6 == 0 else 2

    def gradient(layer, d, x):
        d[pl.ds(0, HALO)] = blank16
        d[pl.ds(HALO + rows, HALO)] = blank16

        def one(m, total):
            which = [1 + many * m + k for k in range(many)]
            left, right = [], []
            for p in which:
                for e in (2 * p, 2 * p + 1):
                    left.append(jnp.concatenate([d[e + 1], d[e], d[e - 1]], axis=0))
                right.append(x[p])
            return total + lax.dot_general(
                jnp.concatenate(left, axis=1), jnp.concatenate(right, axis=1),
                (((1,), (1,)), ((), ())), preferred_element_type=F32)
        grad[layer] = lax.fori_loop(
            0, (pairs - 2) // many, one, jnp.zeros((3 * ch, 3 * ch), F32))
        for i in range(1, ns):
            g_copy(layer, i, space).start()

    def part(index):
        return pl.ds(pl.multiple_of(index * quarter, quarter), quarter)

    def g_copy(layer, i, source):
        k = neighbour(i)
        return pltpu.make_async_remote_copy(
            src_ref=grad.at[layer, part(k)], dst_ref=grecv.at[layer, source],
            send_sem=g_send.at[layer, k], recv_sem=g_recv.at[layer, source],
            device_id={"space": k}, device_id_type=MESH)

    def r_copy(layer, i, source):
        k = neighbour(i)
        return pltpu.make_async_remote_copy(
            src_ref=gsum.at[layer, part(source)], dst_ref=gsum.at[layer, part(source)],
            send_sem=r_send.at[layer, k], recv_sem=r_recv.at[layer, source],
            device_id={"space": k}, device_id_type=MESH)

    def reduce_part(layer):
        total = grad[layer, part(space)]
        for i in range(1, ns):
            g_copy(layer, i, neighbour(i)).wait_recv()
            total = total + grecv[layer, neighbour(i)]
        gsum[layer, part(space)] = total
        for i in range(1, ns):
            r_copy(layer, i, space).start()

    def collect(layer):
        for i in range(1, ns):
            g_copy(layer, i, space).wait_send()
            r_copy(layer, i, neighbour(i)).wait_recv()
            r_copy(layer, i, space).wait_send()
        for ty in range(3):
            for tx in range(3):
                gout[9 * layer + 3 * ty + tx] = (
                    gsum[layer, ty * ch:(ty + 1) * ch, tx * ch:(tx + 1) * ch])

    def last_steps(settle, rim):
        gradient(1, d1, x1)
        settle()
        rim()

        def scale(p):
            for e in (2 * p, 2 * p + 1):
                after = a[e] + gathered(y0, e)
                a1[e] = after
                d0[e] = jnp.where(inside(e), scaled(t0[e], after), 0.0).astype(BF16)

        def scale_some(m):
            for k in range(many):
                scale(1 + many * m + k)
        loop(0, (pairs - 2) // many, scale_some)
        top, bottom = d0[HALO - 1], d0[HALO + rows]
        gradient(0, d0, x0)
        d0[HALO - 1] = top
        d0[HALO + rows] = bottom

        wait_x_sent(3)
        reduce_part(1)

        def second(m):
            convolve([1 + many * m + k for k in range(many)],
                     lambda e: d0[e].astype(F32), wb.at[0], y1)
        loop(0, (pairs - 2) // many, second)
        reduce_part(0)

        def end(m):
            for e in range(4):
                at = HALO + 4 * m + e
                a1[at] = a1[at] + gathered(y1, at)
        loop(0, rows // 4, end)

    sweep(3, False, None, adjoint_first(3, a, True), wb.at[1], None, None, None, last=last_steps)
    for r in range(rows):
        pltpu.make_async_copy(a1.at[HALO + r], adj_out.at[:, r, 0], out_sem.at[1]).start()
    collect(1)
    collect(0)
    grads = pltpu.make_async_copy(gout, grads_out, out_sem.at[2])
    grads.start()
    pltpu.make_async_copy(own_rows(s), own_rows(s), out_sem.at[0]).wait()
    pltpu.make_async_copy(own_rows(a1), own_rows(a1), out_sem.at[1]).wait()
    grads.wait()


def publish_body(*refs):
    half = len(refs) // 2
    for source, target in zip(refs[:half], refs[half:]):
        target[...] = source[...]


def publish(*arrays):
    steps = 2
    specs = [
        pl.BlockSpec((x.shape[0] // steps,) + x.shape[1:], lambda i, n=x.ndim: (i,) + (0,) * (n - 1))
        for x in arrays]
    return pl.pallas_call(
        publish_body,
        grid=(steps,),
        out_shape=tuple(jax.ShapeDtypeStruct(x.shape, x.dtype) for x in arrays),
        in_specs=specs,
        out_specs=tuple(specs),
        name="publish",
    )(*arrays)


def per_device(image_features, output_cotangent, conv_weights):
    nl, ns = lax.axis_size("layer"), lax.axis_size("space")
    layers, _, ch, _ = conv_weights.shape
    _, _, rows, cols = image_features.shape
    assert rows == nl and layers == 2 and cols == 2 * ch
    step_size = HORIZON / (layers * nl)
    ext = rows + 2 * HALO
    vmem = pltpu.VMEM

    def field(kind):
        return vmem((ext, ch, cols), kind)
    any_spec = pl.BlockSpec(memory_space=pl.ANY)
    dma = pltpu.SemaphoreType.DMA
    phases = 2 * ITERS
    states, starts, grads = pl.pallas_call(
        functools.partial(kernel, nl, ns, rows, ch, cols, step_size),
        out_shape=(
            jax.ShapeDtypeStruct((ch, rows, 1, cols), F32),
            jax.ShapeDtypeStruct((ch, rows, 1, cols), F32),
            jax.ShapeDtypeStruct((layers * 9, ch, ch), F32),
        ),
        in_specs=[any_spec, any_spec, any_spec],
        out_specs=(any_spec, any_spec, any_spec),
        scratch_shapes=[
            field(F32), field(F32), field(F32), field(F32), field(F32), field(F32), field(F32),
            vmem((ext + 2, 3 * ch, cols), F32),
            vmem((ext + 2, 3 * ch, cols), F32),
            vmem((ext // 2, 3 * ch, 2 * cols), BF16),
            vmem((ext // 2, 3 * ch, 2 * cols), BF16),
            field(BF16), field(BF16),
            vmem((phases, rows, ch, cols), BF16),
            vmem((phases, nl, ch, cols), BF16),
            vmem((phases, nl, ch, cols), BF16),
            vmem((phases, ext, ch, cols), BF16),
            vmem((layers, 9, ch, ch), BF16),
            vmem((layers, 3 * ch, 3 * ch), BF16),
            vmem((layers, 3 * ch, 3 * ch), BF16),
            vmem((nl, ch, 2 * ch), BF16),
            vmem((nl, ch, 2 * ch), BF16),
            vmem((nl // GROUP, (GROUP + 2) * ch, 2 * ch), BF16),
            vmem((nl // GROUP, (GROUP + 2) * ch, 2 * ch), BF16),
            vmem((nl, ch, cols), F32),
            vmem((layers, 3 * ch, 3 * ch), F32),
            vmem((layers, ns, 3 * ch // ns, 3 * ch), F32),
            vmem((layers, 3 * ch, 3 * ch), F32),
            vmem((layers * 9, ch, ch), F32),
            dma((3,)), dma((3,)), dma((4,)), dma((4,)), dma((2,)), dma((2,)),
            dma((nl,)), dma((nl,)),
            dma((nl,)), dma((phases, nl)), dma((nl,)), dma((phases, nl)),
            dma((phases, 4)), dma((phases, 4)),
            dma((layers, ns)), dma((layers, ns)), dma((layers, ns)), dma((layers, ns)),
        ],
        compiler_params=pltpu.CompilerParams(
            collective_id=0, has_side_effects=True, vmem_limit_bytes=56 * 1024 * 1024),
        name="mgrit",
    )(
        image_features.reshape(ch, rows, 1, cols),
        output_cotangent.reshape(ch, rows, 1, cols),
        conv_weights,
    )
    states, starts, grads = publish(
        states.reshape(ch * rows, cols), starts.reshape(ch * rows, cols),
        grads.reshape(layers * 9 * ch, ch))
    return (
        states.reshape(1, 1, ch, rows, cols),
        starts.reshape(1, 1, ch, rows, cols),
        grads.reshape(layers, 9, ch, ch),
    )


def solution(mesh):
    placed = (
        P(None, None, "space", None),
        P(None, None, "space", None),
        P("layer", None, None, None),
    )
    return jax.shard_map(
        per_device,
        mesh=mesh,
        in_specs=placed,
        out_specs=(
            P("layer", None, None, "space", None),
            P("layer", None, None, "space", None),
            P("layer", None, None, None),
        ),
        check_vma=False,
    )
```
